512 devices in a mesh: bx: 32 (over x_hi, z), by: 16 (over x_lo, y, core).
Axes of the slice: x: 4 (x_hi: 2, x_lo: 2; x = x_hi * 2 + x_lo), y: 4, z: 16, core: 2. Of those that a mesh axis runs over, the one named last changes fastest.
Arguments:
- charges: float32 [32, 16, 2048, 128], P('bx', 'by'), may hold values from -6 to 6
- speed: float32 [32, 16, 2048], P('bx', 'by'), may hold values from 0.5 to 2
- omega: float32 [4, 64], replicated, may hold values from -3.140625 to 3.140625
- mixers: float32 [4, 2, 2, 128, 128], replicated, may hold values from -0.375 to 0.375
- source_map: float32 [128, 128], replicated, may hold values from -0.5 to 0.5
- target_map: float32 [128, 1024], replicated, may hold values from -0.5 to 0.5
Outputs:
- targets: bfloat16 [32, 16, 2048, 1024], P('bx', 'by')
The draws below stay inside these ranges and needn't reach their ends.
All inputs are finite; a program needn't handle non-finite values.
Results may differ from the reference program's by a relative error of at most 0.001.
Values sent between devices are 32-bit elements; how exact they have to be, the bound alone decides.
A program may use at most 64 MiB of HBM per device.

```python
import math
import jax
import jax.numpy as jnp
from jax import lax

RANK = 64
LEVELS = 4
BOXES_DEV = 2048
SRC = 128
TGT = 1024
N_BX = 32
N_BY = 16


def shard_levels(own_key, shape, pieces, smallest, largest):
    def one(dim, blocks):
        draws = jax.random.uniform(jax.random.fold_in(jax.random.fold_in(own_key, 6), dim), (blocks,), jnp.float32, smallest / len(pieces), largest / len(pieces))
        return jnp.repeat(jnp.exp(draws), shape[dim] // blocks).reshape((-1,) + (1,) * (len(shape) - dim - 1))

    level = one(*pieces[0])
    for cut in pieces[1:]:
        level = level * one(*cut)
    return level


def noise(own_key, dims, spread, most, cuts=(), dtype=jnp.bfloat16):
    drawn = jax.random.normal(own_key, dims, jnp.float32) * spread
    if len(cuts) > 0:
        drawn = shard_levels(own_key, dims, cuts, -0.22, 0.18) * drawn
    return jnp.clip(drawn, min=-most, max=most).astype(dtype)


def setup_inputs(seed: int = 0) -> dict:
    streams_of = jax.random.split(jax.random.key(seed), 7)
    return {
        "charges": noise(streams_of[0], (N_BX, N_BY, BOXES_DEV, SRC), 1.0, 6.0, ((0, 32), (1, 16)), jnp.float32),
        "speed": jnp.clip(jnp.exp(math.log(2.0) - 1.3862944 * jax.random.uniform(streams_of[1], (N_BX, N_BY, BOXES_DEV), jnp.float32) ** shard_levels(streams_of[1], (N_BX, N_BY, BOXES_DEV), ((0, 32), (1, 16)), -0.2, 0.2)), 0.5, 2.0),
        "omega": jnp.clip(jax.random.uniform(streams_of[2], (LEVELS, RANK), jnp.float32, -3.140625, 3.140625), -3.140625, 3.140625),
        "mixers": noise(streams_of[3], (LEVELS, 2, 2, 2 * RANK, 2 * RANK), (4 * RANK) ** -0.5, 0.375, (), jnp.float32),
        "source_map": noise(streams_of[4], (SRC, 2 * RANK), SRC ** -0.5, 0.5, (), jnp.float32),
        "target_map": noise(streams_of[5], (2 * RANK, TGT), (2 * RANK) ** -0.5, 0.5, (), jnp.float32),
    }


HIGH = lax.Precision.HIGHEST


def rotate(weights, angles):
    half = weights.shape[-1] // 2
    real_part = weights[..., :half]
    imag_part = weights[..., half:]
    cosine = jnp.cos(angles)
    sine = jnp.sin(angles)
    return jnp.concatenate([real_part * cosine - imag_part * sine, real_part * sine + imag_part * cosine], axis=-1)


def merge_level(rotated, level_mix, axis, parity):
    moved = jnp.moveaxis(rotated, axis, 0)
    count = moved.shape[0]
    bit = 0 if parity == 0 else count.bit_length() - 2
    stride = 2 ** bit
    grouped = moved.reshape((count // (2 * stride), 2, stride) + moved.shape[1:])
    child_zero = grouped[:, 0]
    child_one = grouped[:, 1]
    new_zero = jnp.matmul(child_zero, level_mix[0, 0], precision=HIGH) + jnp.matmul(child_one, level_mix[0, 1], precision=HIGH)
    new_one = jnp.matmul(child_zero, level_mix[1, 0], precision=HIGH) + jnp.matmul(child_one, level_mix[1, 1], precision=HIGH)
    stacked = jnp.stack([new_zero, new_one], axis=1).reshape(moved.shape)
    return jnp.moveaxis(stacked, 0, axis)


def reference(charges, speed, omega, mixers, source_map, target_map):
    weights = jnp.matmul(charges, source_map, precision=HIGH)
    half_levels = LEVELS // 2
    for level in range(LEVELS):
        axis = 0 if level < half_levels else 1
        parity = level % half_levels
        angles = speed[..., None] * omega[level]
        weights = merge_level(rotate(weights, angles), mixers[level], axis, parity)
    return jnp.matmul(weights, target_map, precision=HIGH).astype(jnp.bfloat16)
```

```python
import functools
import math

import jax
import jax.numpy as jnp
from jax import lax
from jax.experimental import pallas as pl
from jax.experimental.pallas import tpu as pltpu
from jax.sharding import PartitionSpec as P

MESH = pl.DeviceIdType.MESH
LANES = 128
HALF = 64
GROUP = 8
CHUNKS = 8
F32 = jnp.float32
BF16 = jnp.bfloat16


def sine_coefficients(terms):
    import numpy as np

    points = 0.5 * np.cos((np.arange(2000) + 0.5) / 2000 * np.pi / 2)
    basis = np.stack([points ** (2 * k + 1) for k in range(terms)], axis=1)
    solved = np.linalg.lstsq(basis, np.sin(2 * np.pi * points), rcond=None)[0]
    return [float(value) for value in solved]


SINE = sine_coefficients(7)


def split(value):
    high = value.astype(BF16)
    return high, (value - high.astype(F32)).astype(BF16)


def dot(left, right):
    return jnp.dot(left, right, preferred_element_type=F32)


def phase_tables(speed, turns):
    lane = lax.broadcasted_iota(jnp.int32, speed.shape, 1)
    first = lane < HALF
    angle = speed * turns + jnp.where(first, 0.25, 0.0)
    rest = angle - jnp.round(angle)
    square = rest * rest
    total = jnp.full_like(rest, SINE[-1])
    for term in SINE[-2::-1]:
        total = total * square + term
    wave = total * rest
    turned = pltpu.roll(wave, HALF, 1)
    return jnp.where(first, wave, turned), jnp.where(first, -turned, wave)


def rotate(weights, cosine, sine):
    return weights * cosine + pltpu.roll(weights, HALF, 1) * sine


def butterfly_kernel(
    rows, charges_hbm, speed_hbm, omega_hbm, mixers_hbm, source_hbm, out_hbm,
    charges, speed, omega, mixers, source, speeds, source_pair, first_pair, high_mix, low_mix,
    own_cos, own_sin, cos_tables, sin_tables, z_send, z_recv, a_send, a_recv, b_send,
    load_sem, speed_sems, z_send_sems, z_recv_sems, a_send_sem, a_recv_sems, b_send_sem, b_recv_sem, own_sem,
):
    block = rows // GROUP // CHUNKS
    per_peer = rows // GROUP
    bx, by = lax.axis_index("bx"), lax.axis_index("by")
    z_count = lax.axis_size("bx") // 2
    y_count = lax.axis_size("by") // 2
    side = lax.rem(bx, 2)
    x_hi, x_lo, core = bx // z_count, by // y_count, lax.rem(by, 2)
    me = x_hi * 4 + core * 2 + x_lo

    loads = [
        pltpu.make_async_copy(speed_hbm, speed, load_sem.at[0]),
        pltpu.make_async_copy(omega_hbm, omega, load_sem.at[1]),
        pltpu.make_async_copy(charges_hbm, charges, load_sem.at[2]),
        pltpu.make_async_copy(source_hbm, source, load_sem.at[3]),
        pltpu.make_async_copy(mixers_hbm, mixers, load_sem.at[4]),
    ]
    for load in loads:
        load.start()

    z_peer = {"bx": bx + 1 - 2 * side}
    peers = []
    for mask in range(1, GROUP):
        other_hi = lax.rem(x_hi + mask // 4, 2)
        other_core = lax.rem(core + mask // 2 % 2, 2)
        other_lo = lax.rem(x_lo + mask % 2, 2)
        device = {
            "bx": other_hi * z_count + lax.rem(bx, z_count),
            "by": other_lo * y_count + (lax.rem(by, y_count) // 2) * 2 + other_core,
        }
        peers.append((device, other_hi * 4 + other_core * 2 + other_lo))

    barrier = pltpu.get_barrier_semaphore()
    pl.semaphore_signal(barrier, inc=1, device_id=z_peer, device_id_type=MESH)
    for device, _ in peers:
        pl.semaphore_signal(barrier, inc=1, device_id=device, device_id_type=MESH)

    def column(row):
        return jnp.transpose(jnp.broadcast_to(row, (LANES, LANES)))

    halves = per_peer // LANES
    loads[0].wait()
    loads[1].wait()

    def turns_of(level):
        return omega[pl.ds(level, 1), :] * (1.0 / (2.0 * math.pi))

    def own_tables(step, carry):
        half, place = step // GROUP, lax.rem(step, GROUP)
        cosine, sine = phase_tables(column(speed[place, pl.ds(half, 1), :]), turns_of(0))
        span = pl.ds(pl.multiple_of(half * LANES, LANES), LANES)
        own_cos[place, span, :] = cosine
        own_sin[place, span, :] = sine
        return carry

    lax.fori_loop(0, halves * GROUP, own_tables, 0)

    loads[3].wait()
    high, low = split(source[...])
    source_pair[0:LANES, 0:LANES] = high
    source_pair[0:LANES, LANES:] = low
    source_pair[LANES:, 0:LANES] = high
    source_pair[LANES:, LANES:] = jnp.zeros_like(high)
    loads[2].wait()

    def span_of(chunk):
        return pl.ds(pl.multiple_of(chunk * block, block), block)

    def start(chunk):
        span = span_of(chunk)
        high, low = split(charges[:, span, :].reshape(GROUP * block, LANES))
        both = dot(jnp.concatenate([high, low], axis=1), source_pair[...])
        weights = both[:, :LANES] + both[:, LANES:]
        cosine = own_cos[:, span, :].reshape(GROUP * block, LANES)
        sine = own_sin[:, span, :].reshape(GROUP * block, LANES)
        z_send[chunk] = rotate(weights, cosine, sine).reshape(GROUP, block, LANES)

    def z_copy(chunk):
        return pltpu.make_async_remote_copy(
            src_ref=z_send.at[chunk], dst_ref=z_recv.at[chunk],
            send_sem=z_send_sems.at[chunk], recv_sem=z_recv_sems.at[chunk],
            device_id=z_peer, device_id_type=MESH,
        )

    start(0)
    pl.semaphore_wait(barrier, GROUP)
    z_copy(0).start()
    for device, place in peers:
        pltpu.make_async_remote_copy(
            src_ref=speed.at[place], dst_ref=speeds.at[me],
            send_sem=speed_sems.at[0], recv_sem=speed_sems.at[1],
            device_id=device, device_id_type=MESH,
        ).start()

    def start_and_send(chunk, carry):
        start(chunk)
        z_copy(chunk).start()
        return carry

    lax.fori_loop(1, CHUNKS, start_and_send, 0)

    loads[4].wait()
    for child in range(2):
        high, low = split(mixers[0, side, lax.rem(side + child, 2)])
        first_pair[child * LANES:(child + 1) * LANES, 0:LANES] = high
        first_pair[child * LANES:(child + 1) * LANES, LANES:] = low
        for level in range(1, 4):
            for target in range(2):
                high, low = split(mixers[level, target, child])
                place = (level - 1, slice(child * LANES, (child + 1) * LANES), slice(target * LANES, (target + 1) * LANES))
                high_mix[place] = high
                low_mix[place] = low

    def wait_bytes(ref, sem):
        pltpu.make_async_copy(ref, ref, sem).wait()

    speeds[me] = speed[me]
    wait_bytes(speeds.at[pl.ds(0, GROUP - 1)], speed_sems.at[1])

    def group_tables(step, carry):
        half, place = step // GROUP, lax.rem(step, GROUP)
        wide = column(speeds[place, pl.ds(half, 1), :])
        span = pl.ds(pl.multiple_of(half * LANES, LANES), LANES)
        for level in range(1, 4):
            cosine, sine = phase_tables(wide, turns_of(level))
            cos_tables[level - 1, place, span, :] = cosine
            sin_tables[level - 1, place, span, :] = sine
        return carry

    lax.fori_loop(0, halves * GROUP, group_tables, 0)

    def first_level(chunk):
        z_copy(chunk).wait_recv()
        own = z_send[chunk].reshape(GROUP * block, LANES)
        other = z_recv[chunk].reshape(GROUP * block, LANES)
        high, low = split(jnp.concatenate([own, other], axis=1))
        both = dot(high, first_pair[...])
        total = both[:, :LANES] + both[:, LANES:] + dot(low, first_pair[:, :LANES])
        a_send[chunk] = total.reshape(GROUP, block, LANES)
        for device, place in peers:
            pltpu.make_async_remote_copy(
                src_ref=a_send.at[chunk, place], dst_ref=a_recv.at[chunk, me],
                send_sem=a_send_sem, recv_sem=a_recv_sems.at[chunk],
                device_id=device, device_id_type=MESH,
            ).start()
        a_recv[chunk, me] = a_send[chunk, me]

    def other_levels(chunk):
        wait_bytes(a_recv.at[chunk, pl.ds(0, GROUP - 1)], a_recv_sems.at[chunk])
        span = span_of(chunk)
        weights = a_recv[chunk].reshape(GROUP * block, LANES)
        for level in range(1, 4):
            cosine = cos_tables[level - 1, :, span, :].reshape(GROUP * block, LANES)
            sine = sin_tables[level - 1, :, span, :].reshape(GROUP * block, LANES)
            rotated = rotate(weights, cosine, sine)
            stride = {1: 4, 2: 2, 3: 1}[level]
            low_places = [place for place in range(GROUP) if place // stride % 2 == 0]

            def rows_of(place):
                return rotated[place * block:(place + 1) * block]

            pairs = jnp.concatenate(
                [
                    jnp.concatenate([rows_of(place) for place in low_places], axis=0),
                    jnp.concatenate([rows_of(place + stride) for place in low_places], axis=0),
                ],
                axis=1,
            )
            high, low = split(pairs)
            both = dot(jnp.concatenate([high, low], axis=0), high_mix[level - 1])
            count = pairs.shape[0]
            mixed = both[:count] + both[count:] + dot(high, low_mix[level - 1])
            parts = [None] * GROUP
            for index, place in enumerate(low_places):
                taken = mixed[index * block:(index + 1) * block]
                parts[place] = taken[:, :LANES]
                parts[place + stride] = taken[:, LANES:]
            weights = jnp.concatenate(parts, axis=0)
        b_send[chunk] = weights.reshape(GROUP, block, LANES)
        for device, place in peers:
            pltpu.make_async_remote_copy(
                src_ref=b_send.at[chunk, place], dst_ref=out_hbm.at[me, span],
                send_sem=b_send_sem, recv_sem=b_recv_sem,
                device_id=device, device_id_type=MESH,
            ).start()
        pltpu.make_async_copy(b_send.at[chunk, me], out_hbm.at[me, span], own_sem).start()

    def step(index, carry):
        @pl.when(index < CHUNKS)
        def _():
            first_level(index)

        @pl.when(index > 0)
        def _():
            other_levels(index - 1)

        return carry

    lax.fori_loop(0, CHUNKS + 1, step, 0)

    wait_bytes(out_hbm.at[pl.ds(0, GROUP - 1)], b_recv_sem)
    wait_bytes(out_hbm.at[0], own_sem)
    wait_bytes(out_hbm.at[pl.ds(0, GROUP - 1)], a_send_sem)
    wait_bytes(out_hbm.at[pl.ds(0, GROUP - 1)], b_send_sem)
    wait_bytes(speeds.at[pl.ds(0, GROUP - 1)], speed_sems.at[0])
    for chunk in range(CHUNKS):
        z_copy(chunk).wait_send()


def butterfly(charges, speed, omega, mixers, source_map):
    rows = charges.shape[0]
    per_peer = rows // GROUP
    block = per_peer // CHUNKS
    chunked = (CHUNKS, GROUP, block, LANES)
    whole = (GROUP, per_peer, LANES)
    dma = pltpu.SemaphoreType.DMA
    return pl.pallas_call(
        functools.partial(butterfly_kernel, rows),
        name="butterfly",
        out_shape=jax.ShapeDtypeStruct(whole, F32),
        in_specs=[pl.BlockSpec(memory_space=pl.ANY)] * 5,
        out_specs=pl.BlockSpec(memory_space=pl.ANY),
        scratch_shapes=[
            pltpu.VMEM(whole, F32),
            pltpu.VMEM((GROUP, per_peer // LANES, LANES), F32),
            pltpu.VMEM((4, LANES), F32),
            pltpu.VMEM((4, 2, 2, LANES, LANES), F32),
            pltpu.VMEM((LANES, LANES), F32),
            pltpu.VMEM((GROUP, per_peer // LANES, LANES), F32),
            pltpu.VMEM((2 * LANES, 2 * LANES), BF16),
            pltpu.VMEM((2 * LANES, 2 * LANES), BF16),
            pltpu.VMEM((3, 2 * LANES, 2 * LANES), BF16),
            pltpu.VMEM((3, 2 * LANES, 2 * LANES), BF16),
            pltpu.VMEM(whole, F32),
            pltpu.VMEM(whole, F32),
            pltpu.VMEM((3,) + whole, F32),
            pltpu.VMEM((3,) + whole, F32),
            pltpu.VMEM(chunked, F32),
            pltpu.VMEM(chunked, F32),
            pltpu.VMEM(chunked, F32),
            pltpu.VMEM(chunked, F32),
            pltpu.VMEM(chunked, F32),
            dma((5,)),
            dma((2,)),
            dma((CHUNKS,)),
            dma((CHUNKS,)),
            dma,
            dma((CHUNKS,)),
            dma,
            dma,
            dma,
        ],
        compiler_params=pltpu.CompilerParams(
            collective_id=0, has_side_effects=True, vmem_limit_bytes=32 * 2**20
        ),
    )(
        charges.reshape(whole),
        speed.reshape(GROUP, per_peer // LANES, LANES),
        jnp.concatenate([omega, omega], axis=1),
        mixers,
        source_map,
    )


def target_kernel(weights_ref, map_ref, out_ref, double, lower):
    @pl.when(pl.program_id(0) == 0)
    def _():
        high, low = split(map_ref[...])
        double[0:LANES, :] = high
        double[LANES:, :] = high
        lower[...] = low

    high, low = split(weights_ref[...])
    total = dot(jnp.concatenate([high, low], axis=1), double[...]) + dot(high, lower[...])
    out_ref[...] = total.astype(BF16)


def apply_target(weights, target_map):
    rows, targets = weights.shape[0], target_map.shape[1]
    tile = rows // 8
    return pl.pallas_call(
        target_kernel,
        name="target",
        grid=(rows // tile,),
        out_shape=jax.ShapeDtypeStruct((rows, targets), BF16),
        in_specs=[
            pl.BlockSpec((tile, LANES), lambda i: (i, 0)),
            pl.BlockSpec((LANES, targets), lambda i: (0, 0)),
        ],
        out_specs=pl.BlockSpec((tile, targets), lambda i: (i, 0)),
        scratch_shapes=[pltpu.VMEM((2 * LANES, targets), BF16), pltpu.VMEM((LANES, targets), BF16)],
        compiler_params=pltpu.CompilerParams(vmem_limit_bytes=24 * 2**20),
    )(weights, target_map)


def shards(charges, speed, omega, mixers, source_map, target_map):
    box_count = charges.shape[2]
    weights = butterfly(
        charges.reshape(box_count, charges.shape[3]), speed, omega, mixers, source_map
    )
    result = apply_target(weights.reshape(box_count, LANES), target_map)
    return result.reshape(1, 1, box_count, target_map.shape[1])


def solution(mesh):
    placed = (P("bx", "by", None, None), P("bx", "by", None), P(), P(), P(), P())
    return jax.shard_map(
        shards, mesh=mesh, in_specs=placed, out_specs=P("bx", "by", None, None), check_vma=False
    )
```

```python
import functools
import math

import jax
import jax.numpy as jnp
from jax import lax
from jax.experimental import pallas as pl
from jax.experimental.pallas import tpu as pltpu
from jax.sharding import PartitionSpec as P

MESH = pl.DeviceIdType.MESH
LANES = 128
HALF = 64
GROUP = 8
CHUNKS = 8
Z_FIRST = 2
Z_END = CHUNKS // 2
PEER_ORDER = (1, 5, 4, 3, 7, 6, 2)
VMEM_LIMIT = 60 * 2**20
F32 = jnp.float32
BF16 = jnp.bfloat16


def sine_coefficients(terms):
    import numpy as np

    points = 0.5 * np.cos((np.arange(2000) + 0.5) / 2000 * np.pi / 2)
    basis = np.stack([points ** (2 * k + 1) for k in range(terms)], axis=1)
    solved = np.linalg.lstsq(basis, np.sin(2 * np.pi * points), rcond=None)[0]
    return [float(value) for value in solved]


SINE = sine_coefficients(7)


def split(value):
    high = value.astype(BF16)
    return high, (value - high.astype(F32)).astype(BF16)


def dot(left, right):
    return jnp.dot(left, right, preferred_element_type=F32)


def phase_tables(speed, turns):
    lane = lax.broadcasted_iota(jnp.int32, speed.shape, 1)
    first = lane < HALF
    angle = speed * turns + jnp.where(first, 0.25, 0.0)
    rest = angle - jnp.round(angle)
    square = rest * rest
    total = jnp.full_like(rest, SINE[-1])
    for term in SINE[-2::-1]:
        total = total * square + term
    wave = total * rest
    turned = pltpu.roll(wave, HALF, 1)
    return jnp.where(first, wave, turned), jnp.where(first, -turned, wave)


def rotate(weights, cosine, sine):
    return weights * cosine + pltpu.roll(weights, HALF, 1) * sine


def butterfly_kernel(
    rows, charges_hbm, speed_hbm, omega_hbm, mixers_hbm, source_hbm, out_ref,
    charges, speed, omega, mixers, source, speeds, wide, source_pair, first_pair, high_mix, low_mix,
    tables, z_send, z_recv, a_send, a_recv, b_send,
    load_sems, speed_sems, z_send_sems, z_recv_sems, a_send_sem, a_recv_sems, b_send_sem, b_recv_sem,
):
    per_peer = rows // GROUP
    block = per_peer // CHUNKS
    count = GROUP * block
    bx, by = lax.axis_index("bx"), lax.axis_index("by")
    z_count = lax.axis_size("bx") // 2
    y_count = lax.axis_size("by") // 2
    side = lax.rem(bx, 2)
    x_hi, x_lo, core = bx // z_count, by // y_count, lax.rem(by, 2)
    me = x_hi * 4 + core * 2 + x_lo

    z_peer = {"bx": bx + 1 - 2 * side}
    peers = []
    for mask in PEER_ORDER:
        other_hi = lax.rem(x_hi + mask // 4, 2)
        other_core = lax.rem(core + mask // 2 % 2, 2)
        other_lo = lax.rem(x_lo + mask % 2, 2)
        device = {
            "bx": other_hi * z_count + lax.rem(bx, z_count),
            "by": other_lo * y_count + (lax.rem(by, y_count) // 2) * 2 + other_core,
        }
        peers.append((device, other_hi * 4 + other_core * 2 + other_lo))

    barrier = pltpu.get_barrier_semaphore()
    for device, _ in peers[::-1]:
        pl.semaphore_signal(barrier, inc=1, device_id=device, device_id_type=MESH)
    pl.semaphore_signal(barrier, inc=1, device_id=z_peer, device_id_type=MESH)

    loads = [
        pltpu.make_async_copy(speed_hbm, speed, load_sems.at[0]),
        pltpu.make_async_copy(omega_hbm, omega, load_sems.at[1]),
        pltpu.make_async_copy(source_hbm, source, load_sems.at[2]),
        pltpu.make_async_copy(charges_hbm.at[:, pl.ds(0, Z_FIRST * block)], charges, load_sems.at[3]),
        pltpu.make_async_copy(mixers_hbm, mixers, load_sems.at[4]),
    ]
    for load in loads:
        load.start()

    def wait_bytes(ref, sem):
        pltpu.make_async_copy(ref, ref, sem).wait()

    def span_of(chunk):
        return pl.ds(pl.multiple_of(chunk * block, block), block)

    def turns_of(level):
        row = omega[pl.ds(level, 1), :] * (1.0 / (2.0 * math.pi))
        return jnp.concatenate([row, row], axis=1)

    def source_weights(value):
        high, low = split(value)
        both = dot(jnp.concatenate([high, low], axis=1), source_pair[...])
        return both[:, :LANES] + both[:, LANES:]

    def z_copy(chunk):
        return pltpu.make_async_remote_copy(
            src_ref=z_send.at[chunk], dst_ref=z_recv.at[chunk],
            send_sem=z_send_sems.at[chunk], recv_sem=z_recv_sems.at[chunk],
            device_id=z_peer, device_id_type=MESH,
        )

    def scatter(block_of, chunk):
        for device, place in peers:
            pltpu.make_async_remote_copy(
                src_ref=block_of(place), dst_ref=a_recv.at[chunk, me],
                send_sem=a_send_sem, recv_sem=a_recv_sems.at[chunk],
                device_id=device, device_id_type=MESH,
            ).start()
        pltpu.make_async_copy(block_of(me), a_recv.at[chunk, me], a_recv_sems.at[chunk]).start()

    def give_back(chunk):
        span = span_of(chunk)
        for device, place in peers:
            pltpu.make_async_remote_copy(
                src_ref=b_send.at[chunk, place], dst_ref=out_ref.at[me, span],
                send_sem=b_send_sem, recv_sem=b_recv_sem,
                device_id=device, device_id_type=MESH,
            ).start()
        pltpu.make_async_copy(b_send.at[chunk, me], out_ref.at[me, span], b_recv_sem).start()

    loads[0].wait()
    columns = jnp.transpose(speed[:, 0, :])
    own_speed = [
        jnp.concatenate(
            [
                jnp.broadcast_to(columns[chunk * block:(chunk + 1) * block, place:place + 1], (block, LANES))
                for place in range(GROUP)
            ],
            axis=0,
        )
        for chunk in range(Z_FIRST)
    ]
    loads[1].wait()
    loads[2].wait()
    high, low = split(source[...])
    source_pair[0:LANES, 0:LANES] = high
    source_pair[0:LANES, LANES:] = low
    source_pair[LANES:, 0:LANES] = high
    source_pair[LANES:, LANES:] = jnp.zeros_like(high)
    loads[3].wait()
    for chunk in range(Z_FIRST):
        cosine, sine = phase_tables(own_speed[chunk], turns_of(0))
        weights = source_weights(charges[:, chunk * block:(chunk + 1) * block, :].reshape(count, LANES))
        z_send[chunk] = rotate(weights, cosine, sine).reshape(GROUP, block, LANES)
        if chunk == 0:
            pl.semaphore_wait(barrier, GROUP)
            z_copy(0).start()
            for device, place in peers:
                pltpu.make_async_remote_copy(
                    src_ref=speed.at[place], dst_ref=speeds.at[me],
                    send_sem=speed_sems.at[0], recv_sem=speed_sems.at[1],
                    device_id=device, device_id_type=MESH,
                ).start()

            def scatter_charges(later, carry):
                scatter(lambda place: charges_hbm.at[place, span_of(later)], later)
                return carry

            lax.fori_loop(Z_FIRST, CHUNKS, scatter_charges, 0)
        else:
            z_copy(chunk).start()

    speeds[me] = speed[me]
    loads[4].wait()
    for child in range(2):
        high, low = split(mixers[0, side, lax.rem(side + child, 2)])
        first_pair[child * LANES:(child + 1) * LANES, 0:LANES] = high
        first_pair[child * LANES:(child + 1) * LANES, LANES:] = low
        for level in range(1, 4):
            for target in range(2):
                high, low = split(mixers[level, target, child])
                place = (level - 1, slice(child * LANES, (child + 1) * LANES), slice(target * LANES, (target + 1) * LANES))
                high_mix[place] = high
                low_mix[place] = low

    wait_bytes(speeds.at[pl.ds(0, GROUP - 1)], speed_sems.at[1])
    for half in range(per_peer // LANES):
        columns = jnp.transpose(speeds[:, half, :])
        for place in range(GROUP):
            wide[place, half * LANES:(half + 1) * LANES, :] = jnp.broadcast_to(
                columns[:, place:place + 1], (LANES, LANES)
            )

    def make_tables(chunk):
        speed_here = wide[:, span_of(chunk), :].reshape(count, LANES)
        for level in range(1, 4):
            cosine, sine = phase_tables(speed_here, turns_of(level))
            tables[chunk, level - 1, 0] = cosine
            tables[chunk, level - 1, 1] = sine

    def first_level(chunk):
        own = z_send[chunk].reshape(count, LANES)
        other = z_recv[chunk].reshape(count, LANES)
        high, low = split(jnp.concatenate([own, other], axis=1))
        both = dot(high, first_pair[...])
        return both[:, :LANES] + both[:, LANES:] + dot(low, first_pair[:, :LANES])

    def other_levels(chunk, weights):
        for level in range(1, 4):
            rotated = rotate(weights, tables[chunk, level - 1, 0], tables[chunk, level - 1, 1])
            stride = {1: 4, 2: 2, 3: 1}[level]
            low_places = [place for place in range(GROUP) if place // stride % 2 == 0]

            def rows_of(place):
                return rotated[place * block:(place + 1) * block]

            pairs = jnp.concatenate(
                [
                    jnp.concatenate([rows_of(place) for place in low_places], axis=0),
                    jnp.concatenate([rows_of(place + stride) for place in low_places], axis=0),
                ],
                axis=1,
            )
            high, low = split(pairs)
            both = dot(jnp.concatenate([high, low], axis=0), high_mix[level - 1])
            half = count // 2
            mixed = both[:half] + both[half:] + dot(high, low_mix[level - 1])
            parts = [None] * GROUP
            for index, place in enumerate(low_places):
                taken = mixed[index * block:(index + 1) * block]
                parts[place] = taken[:, :LANES]
                parts[place + stride] = taken[:, LANES:]
            weights = jnp.concatenate(parts, axis=0)
        b_send[chunk] = weights.reshape(GROUP, block, LANES)
        give_back(chunk)

    def x_first_start(chunk):
        speed_here = wide[:, span_of(chunk), :].reshape(count, LANES)
        cosine, sine = phase_tables(speed_here, turns_of(0))
        wait_bytes(a_recv.at[chunk], a_recv_sems.at[chunk])
        weights = source_weights(a_recv[chunk].reshape(count, LANES))
        z_send[chunk] = rotate(weights, cosine, sine).reshape(GROUP, block, LANES)
        z_copy(chunk).start()
        make_tables(chunk)

    def z_first_middle(chunk):
        z_copy(chunk).wait_recv()
        a_send[chunk] = first_level(chunk).reshape(GROUP, block, LANES)
        scatter(lambda place: a_send.at[chunk, place], chunk)

    def z_first_end(chunk):
        wait_bytes(a_recv.at[chunk], a_recv_sems.at[chunk])
        other_levels(chunk, a_recv[chunk].reshape(count, LANES))

    def x_first_end(chunk):
        z_copy(chunk).wait_recv()
        other_levels(chunk, first_level(chunk))

    def early(chunk, carry):
        x_first_start(chunk + Z_FIRST)
        z_first_middle(chunk)
        make_tables(chunk)
        return carry

    def late(chunk, carry):
        @pl.when(chunk < CHUNKS - Z_FIRST)
        def _():
            x_first_start(chunk + Z_FIRST)

        x_first_end(chunk)

        @pl.when((chunk >= Z_END) & (chunk < Z_END + Z_FIRST))
        def _():
            z_first_end(chunk - Z_END)

        return carry

    lax.fori_loop(0, Z_FIRST, early, 0)
    lax.fori_loop(Z_FIRST, CHUNKS, late, 0)

    wait_bytes(out_ref, b_recv_sem)
    most = out_ref.at[pl.ds(0, GROUP - 1)]
    wait_bytes(most, a_send_sem)
    wait_bytes(most, b_send_sem)
    wait_bytes(speeds.at[pl.ds(0, GROUP - 1)], speed_sems.at[0])
    for chunk in range(CHUNKS):
        z_copy(chunk).wait_send()


def butterfly(charges, speed, omega, mixers, source_map):
    rows = charges.shape[0]
    per_peer = rows // GROUP
    block = per_peer // CHUNKS
    chunked = (CHUNKS, GROUP, block, LANES)
    whole = (GROUP, per_peer, LANES)
    lines = (GROUP, per_peer // LANES, LANES)
    dma = pltpu.SemaphoreType.DMA
    return pl.pallas_call(
        functools.partial(butterfly_kernel, rows),
        name="butterfly",
        out_shape=jax.ShapeDtypeStruct(whole, F32),
        in_specs=[pl.BlockSpec(memory_space=pltpu.HBM)] * 5,
        out_specs=pl.BlockSpec(memory_space=pl.ANY),
        scratch_shapes=[
            pltpu.VMEM((GROUP, Z_FIRST * block, LANES), F32),
            pltpu.VMEM(lines, F32),
            pltpu.VMEM((4, HALF), F32),
            pltpu.VMEM((4, 2, 2, LANES, LANES), F32),
            pltpu.VMEM((LANES, LANES), F32),
            pltpu.VMEM(lines, F32),
            pltpu.VMEM(whole, F32),
            pltpu.VMEM((2 * LANES, 2 * LANES), BF16),
            pltpu.VMEM((2 * LANES, 2 * LANES), BF16),
            pltpu.VMEM((3, 2 * LANES, 2 * LANES), BF16),
            pltpu.VMEM((3, 2 * LANES, 2 * LANES), BF16),
            pltpu.VMEM((CHUNKS, 3, 2, GROUP * block, LANES), F32),
            pltpu.VMEM(chunked, F32),
            pltpu.VMEM(chunked, F32),
            pltpu.VMEM((Z_FIRST,) + chunked[1:], F32),
            pltpu.VMEM(chunked, F32),
            pltpu.VMEM(chunked, F32),
            dma((5,)),
            dma((2,)),
            dma((CHUNKS,)),
            dma((CHUNKS,)),
            dma,
            dma((CHUNKS,)),
            dma,
            dma,
        ],
        compiler_params=pltpu.CompilerParams(
            collective_id=0, has_side_effects=True, vmem_limit_bytes=VMEM_LIMIT
        ),
    )(
        charges.reshape(whole),
        speed.reshape(lines),
        omega,
        mixers,
        source_map,
    )


def target_kernel(weights_ref, map_ref, out_ref, double, lower):
    @pl.when(pl.program_id(0) == 0)
    def _():
        high, low = split(map_ref[...])
        double[0:LANES, :] = high
        double[LANES:, :] = high
        lower[...] = low

    high, low = split(weights_ref[...])
    total = dot(jnp.concatenate([high, low], axis=1), double[...]) + dot(high, lower[...])
    out_ref[...] = total.astype(BF16)


def apply_target(weights, target_map):
    rows, targets = weights.shape[0], target_map.shape[1]
    tile = rows // 8
    return pl.pallas_call(
        target_kernel,
        name="target",
        grid=(rows // tile,),
        out_shape=jax.ShapeDtypeStruct((rows, targets), BF16),
        in_specs=[
            pl.BlockSpec((tile, LANES), lambda i: (i, 0)),
            pl.BlockSpec((LANES, targets), lambda i: (0, 0)),
        ],
        out_specs=pl.BlockSpec((tile, targets), lambda i: (i, 0)),
        scratch_shapes=[pltpu.VMEM((2 * LANES, targets), BF16), pltpu.VMEM((LANES, targets), BF16)],
        compiler_params=pltpu.CompilerParams(vmem_limit_bytes=24 * 2**20),
    )(weights, target_map)


def shards(charges, speed, omega, mixers, source_map, target_map):
    box_count = charges.shape[2]
    weights = butterfly(
        charges.reshape(box_count, charges.shape[3]), speed, omega, mixers, source_map
    )
    result = apply_target(weights.reshape(box_count, LANES), target_map)
    return result.reshape(1, 1, box_count, target_map.shape[1])


def solution(mesh):
    placed = (P("bx", "by", None, None), P("bx", "by", None), P(), P(), P(), P())
    return jax.shard_map(
        shards, mesh=mesh, in_specs=placed, out_specs=P("bx", "by", None, None), check_vma=False
    )
```

```python
import functools
import math

import jax
import jax.numpy as jnp
from jax import lax
from jax.experimental import pallas as pl
from jax.experimental.pallas import tpu as pltpu
from jax.sharding import PartitionSpec as P

MESH = pl.DeviceIdType.MESH
LANES = 128
HALF = 64
GROUP = 8
CHUNKS = 8
Z_FIRST = 2
Z_END = 3
LAG = 2
PEER_ORDER = (1, 5, 4, 3, 7, 6, 2)
VMEM_LIMIT = 32 * 2**20
F32 = jnp.float32
BF16 = jnp.bfloat16


def sine_coefficients(terms):
    import numpy as np

    points = 0.5 * np.cos((np.arange(2000) + 0.5) / 2000 * np.pi / 2)
    basis = np.stack([points ** (2 * k + 1) for k in range(terms)], axis=1)
    solved = np.linalg.lstsq(basis, np.sin(2 * np.pi * points), rcond=None)[0]
    return [float(value) for value in solved]


SINE = sine_coefficients(7)


def split(value):
    high = value.astype(BF16)
    return high, (value - high.astype(F32)).astype(BF16)


def dot(left, right):
    return jnp.dot(left, right, preferred_element_type=F32)


def phase_tables(speed, turns):
    lane = lax.broadcasted_iota(jnp.int32, speed.shape, 1)
    first = lane < HALF
    angle = speed * turns + jnp.where(first, 0.25, 0.0)
    rest = angle - jnp.round(angle)
    square = rest * rest
    total = jnp.full_like(rest, SINE[-1])
    for term in SINE[-2::-1]:
        total = total * square + term
    wave = total * rest
    turned = pltpu.roll(wave, HALF, 1)
    return jnp.where(first, wave, turned), jnp.where(first, -turned, wave)


def rotate(weights, cosine, sine):
    return weights * cosine + pltpu.roll(weights, HALF, 1) * sine


def butterfly_kernel(
    rows, charges_hbm, speed_hbm, omega_hbm, mixers_hbm, source_hbm, target_hbm, out_ref,
    charges, omega, mixers, source, target, speeds, z_speeds, wide, source_pair, first_pair, high_mix, low_mix,
    target_pair, target_low, tables, z_raw, z_send, z_recv, a_send, a_recv, b_send, b_recv,
    load_sems, speed_sems, z_send_sem, z_recv_sems, a_send_sem, a_recv_sems, b_send_sem, b_recv_sems,
):
    per_peer = rows // GROUP
    block = per_peer // CHUNKS
    count = GROUP * block
    bx, by = lax.axis_index("bx"), lax.axis_index("by")
    z_count = lax.axis_size("bx") // 2
    y_count = lax.axis_size("by") // 2
    side = lax.rem(bx, 2)
    x_hi, x_lo, core = bx // z_count, by // y_count, lax.rem(by, 2)
    me = x_hi * 4 + core * 2 + x_lo

    z_peer = {"bx": bx + 1 - 2 * side}
    peers = []
    for mask in PEER_ORDER:
        other_hi = lax.rem(x_hi + mask // 4, 2)
        other_core = lax.rem(core + mask // 2 % 2, 2)
        other_lo = lax.rem(x_lo + mask % 2, 2)
        device = {
            "bx": other_hi * z_count + lax.rem(bx, z_count),
            "by": other_lo * y_count + (lax.rem(by, y_count) // 2) * 2 + other_core,
        }
        peers.append((device, other_hi * 4 + other_core * 2 + other_lo))

    barrier = pltpu.get_barrier_semaphore()
    for device, _ in peers[::-1]:
        pl.semaphore_signal(barrier, inc=1, device_id=device, device_id_type=MESH)
    pl.semaphore_signal(barrier, inc=1, device_id=z_peer, device_id_type=MESH)

    loads = [
        pltpu.make_async_copy(speed_hbm.at[me], speeds.at[me], load_sems.at[0]),
        pltpu.make_async_copy(omega_hbm, omega, load_sems.at[1]),
        pltpu.make_async_copy(source_hbm, source, load_sems.at[2]),
        pltpu.make_async_copy(charges_hbm.at[:, pl.ds(0, Z_FIRST * block)], charges, load_sems.at[3]),
        pltpu.make_async_copy(mixers_hbm, mixers, load_sems.at[4]),
        pltpu.make_async_copy(target_hbm, target, load_sems.at[5]),
        pltpu.make_async_copy(speed_hbm, z_speeds.at[0], load_sems.at[6]),
    ]
    for load in loads:
        load.start()

    def wait_bytes(ref, sem):
        pltpu.make_async_copy(ref, ref, sem).wait()

    def span_of(chunk):
        return pl.ds(pl.multiple_of(chunk * block, block), block)

    def turns_of(level):
        row = omega[pl.ds(level, 1), :] * (1.0 / (2.0 * math.pi))
        return jnp.concatenate([row, row], axis=1)

    def source_weights(value):
        high, low = split(value)
        both = dot(jnp.concatenate([high, low], axis=1), source_pair[...])
        return both[:, :LANES] + both[:, LANES:]

    def z_pieces(block_of, into, chunk):
        for place in range(GROUP):
            pltpu.make_async_remote_copy(
                src_ref=block_of(place), dst_ref=into.at[chunk, place],
                send_sem=z_send_sem, recv_sem=z_recv_sems.at[chunk],
                device_id=z_peer, device_id_type=MESH,
            ).start()

    def scatter(block_of, chunk):
        for device, place in peers:
            pltpu.make_async_remote_copy(
                src_ref=block_of(place), dst_ref=a_recv.at[chunk, me],
                send_sem=a_send_sem, recv_sem=a_recv_sems.at[chunk],
                device_id=device, device_id_type=MESH,
            ).start()
        pltpu.make_async_copy(block_of(me), a_recv.at[chunk, me], a_recv_sems.at[chunk]).start()

    def give_back(chunk):
        for device, place in peers:
            pltpu.make_async_remote_copy(
                src_ref=b_send.at[chunk, place], dst_ref=b_recv.at[chunk, me],
                send_sem=b_send_sem, recv_sem=b_recv_sems.at[chunk],
                device_id=device, device_id_type=MESH,
            ).start()
        pltpu.make_async_copy(b_send.at[chunk, me], b_recv.at[chunk, me], b_recv_sems.at[chunk]).start()

    def charges_of(chunk):
        return lambda place: charges_hbm.at[place, span_of(chunk)]

    pl.semaphore_wait(barrier, GROUP)
    z_pieces(charges_of(0), z_raw, 0)
    pltpu.make_async_remote_copy(
        src_ref=speed_hbm, dst_ref=z_speeds.at[1],
        send_sem=speed_sems.at[0], recv_sem=speed_sems.at[1],
        device_id=z_peer, device_id_type=MESH,
    ).start()
    for device, place in peers:
        pltpu.make_async_remote_copy(
            src_ref=speed_hbm.at[place], dst_ref=speeds.at[me],
            send_sem=speed_sems.at[2], recv_sem=speed_sems.at[3],
            device_id=device, device_id_type=MESH,
        ).start()
    scatter(charges_of(Z_FIRST), Z_FIRST)
    for chunk in range(1, Z_FIRST):
        z_pieces(charges_of(chunk), z_raw, chunk)

    def scatter_charges(later, carry):
        scatter(charges_of(later), later)
        return carry

    lax.fori_loop(Z_FIRST + 1, CHUNKS, scatter_charges, 0)

    loads[1].wait()
    loads[2].wait()
    high, low = split(source[...])
    source_pair[0:LANES, 0:LANES] = high
    source_pair[0:LANES, LANES:] = low
    source_pair[LANES:, 0:LANES] = high
    source_pair[LANES:, LANES:] = jnp.zeros_like(high)

    loads[4].wait()
    for child in range(2):
        high, low = split(mixers[0, side, lax.rem(side + child, 2)])
        first_pair[child * LANES:(child + 1) * LANES, 0:LANES] = high
        first_pair[child * LANES:(child + 1) * LANES, LANES:] = low
        for level in range(1, 4):
            for half in range(2):
                high, low = split(mixers[level, half, child])
                place = (level - 1, slice(child * LANES, (child + 1) * LANES), slice(half * LANES, (half + 1) * LANES))
                high_mix[place] = high
                low_mix[place] = low

    loads[0].wait()
    wait_bytes(speeds.at[pl.ds(0, GROUP - 1)], speed_sems.at[3])
    for half in range(per_peer // LANES):
        columns = jnp.transpose(speeds[:, half, :])
        for place in range(GROUP):
            wide[place, half * LANES:(half + 1) * LANES, :] = jnp.broadcast_to(
                columns[:, place:place + 1], (LANES, LANES)
            )

    loads[3].wait()
    loads[6].wait()
    wait_bytes(z_speeds.at[1], speed_sems.at[1])

    def make_tables(chunk):
        speed_here = wide[:, span_of(chunk), :].reshape(count, LANES)
        for level in range(1, 4):
            cosine, sine = phase_tables(speed_here, turns_of(level))
            tables[chunk, level - 1, 0] = cosine
            tables[chunk, level - 1, 1] = sine

    def first_level(own, other):
        high, low = split(jnp.concatenate([own, other], axis=1))
        both = dot(high, first_pair[...])
        return both[:, :LANES] + both[:, LANES:] + dot(low, first_pair[:, :LANES])

    def other_levels(chunk, weights):
        for level in range(1, 4):
            rotated = rotate(weights, tables[chunk, level - 1, 0], tables[chunk, level - 1, 1])
            stride = {1: 4, 2: 2, 3: 1}[level]
            low_places = [place for place in range(GROUP) if place // stride % 2 == 0]

            def rows_of(place):
                return rotated[place * block:(place + 1) * block]

            pairs = jnp.concatenate(
                [
                    jnp.concatenate([rows_of(place) for place in low_places], axis=0),
                    jnp.concatenate([rows_of(place + stride) for place in low_places], axis=0),
                ],
                axis=1,
            )
            high, low = split(pairs)
            both = dot(jnp.concatenate([high, low], axis=0), high_mix[level - 1])
            half = count // 2
            mixed = both[:half] + both[half:] + dot(high, low_mix[level - 1])
            parts = [None] * GROUP
            for index, place in enumerate(low_places):
                taken = mixed[index * block:(index + 1) * block]
                parts[place] = taken[:, :LANES]
                parts[place + stride] = taken[:, LANES:]
            weights = jnp.concatenate(parts, axis=0)
        b_send[chunk] = weights.reshape(GROUP, block, LANES)
        give_back(chunk)

    def x_first_start(chunk):
        speed_here = wide[:, span_of(chunk), :].reshape(count, LANES)
        cosine, sine = phase_tables(speed_here, turns_of(0))
        wait_bytes(a_recv.at[chunk], a_recv_sems.at[chunk])
        weights = source_weights(a_recv[chunk].reshape(count, LANES))
        z_send[chunk] = rotate(weights, cosine, sine).reshape(GROUP, block, LANES)
        z_pieces(lambda place: z_send.at[chunk, place], z_recv, chunk)

    def z_first_middle(chunk):
        wait_bytes(z_raw.at[chunk], z_recv_sems.at[chunk])
        turns = turns_of(0)
        sides = []
        for index, value in enumerate((charges[:, chunk * block:(chunk + 1) * block, :], z_raw[chunk])):
            columns = jnp.transpose(z_speeds[index, :, 0, :])
            speed_here = jnp.concatenate(
                [
                    jnp.broadcast_to(columns[chunk * block:(chunk + 1) * block, place:place + 1], (block, LANES))
                    for place in range(GROUP)
                ],
                axis=0,
            )
            cosine, sine = phase_tables(speed_here, turns)
            sides.append(rotate(source_weights(value.reshape(count, LANES)), cosine, sine))
        a_send[chunk] = first_level(*sides).reshape(GROUP, block, LANES)
        scatter(lambda place: a_send.at[chunk, place], chunk)

    def z_first_end(chunk):
        wait_bytes(a_recv.at[chunk], a_recv_sems.at[chunk])
        other_levels(chunk, a_recv[chunk].reshape(count, LANES))

    def x_first_end(chunk):
        wait_bytes(z_recv.at[chunk], z_recv_sems.at[chunk])
        other_levels(chunk, first_level(z_send[chunk].reshape(count, LANES), z_recv[chunk].reshape(count, LANES)))

    def targets(chunk):
        wait_bytes(b_recv.at[chunk], b_recv_sems.at[chunk])
        high, low = split(b_recv[chunk].reshape(count, LANES))
        both = jnp.concatenate([high, low], axis=1)
        width = 2 * LANES
        for column in range(0, out_ref.shape[2], width):
            here = slice(column, column + width)
            total = dot(both, target_pair[:, here]) + dot(high, target_low[:, here])
            out_ref[:, span_of(chunk), here] = total.astype(BF16).reshape(GROUP, block, width)

    for chunk in range(Z_FIRST):
        x_first_start(chunk + Z_FIRST)
        z_first_middle(chunk)
        make_tables(chunk)
        make_tables(chunk + Z_FIRST)
    loads[5].wait()
    high, low = split(target[...])
    target_pair[0:LANES, :] = high
    target_pair[LANES:, :] = high
    target_low[...] = low

    def late(chunk, carry):
        @pl.when(chunk < CHUNKS - Z_FIRST)
        def _():
            x_first_start(chunk + Z_FIRST)
            make_tables(chunk + Z_FIRST)

        @pl.when((chunk >= Z_END) & (chunk < Z_END + Z_FIRST))
        def _():
            z_first_end(chunk - Z_END)

        @pl.when((chunk >= Z_END + LAG) & (chunk < Z_END + LAG + Z_FIRST))
        def _():
            targets(chunk - Z_END - LAG)

        @pl.when(chunk >= Z_FIRST + LAG)
        def _():
            targets(chunk - LAG)

        x_first_end(chunk)
        return carry

    lax.fori_loop(Z_FIRST, CHUNKS, late, 0)

    def finish(chunk, carry):
        targets(chunk)
        return carry

    lax.fori_loop(CHUNKS - LAG, CHUNKS, finish, 0)

    most = wide.at[pl.ds(0, GROUP - 1)]
    wait_bytes(wide, z_send_sem)
    wait_bytes(most, a_send_sem)
    wait_bytes(most, b_send_sem)
    wait_bytes(z_speeds.at[1], speed_sems.at[0])
    wait_bytes(speeds.at[pl.ds(0, GROUP - 1)], speed_sems.at[2])


def shards(charges, speed, omega, mixers, source_map, target_map):
    rows, targets = charges.shape[2], target_map.shape[1]
    per_peer = rows // GROUP
    block = per_peer // CHUNKS
    chunked = (CHUNKS, GROUP, block, LANES)
    first = (Z_FIRST, GROUP, block, LANES)
    whole = (GROUP, per_peer, LANES)
    lines = (GROUP, per_peer // LANES, LANES)
    dma = pltpu.SemaphoreType.DMA
    operands = [charges.reshape(whole), speed.reshape(lines), omega, mixers, source_map, target_map]
    result = pl.pallas_call(
        functools.partial(butterfly_kernel, rows),
        name="butterfly",
        out_shape=pltpu.VMEM((GROUP, per_peer, targets), BF16),
        in_specs=[pl.BlockSpec(memory_space=pltpu.HBM)] * len(operands),
        out_specs=pl.BlockSpec(memory_space=pltpu.VMEM),
        scratch_shapes=[
            pltpu.VMEM((GROUP, Z_FIRST * block, LANES), F32),
            pltpu.VMEM((4, HALF), F32),
            pltpu.VMEM((4, 2, 2, LANES, LANES), F32),
            pltpu.VMEM((LANES, LANES), F32),
            pltpu.VMEM((LANES, targets), F32),
            pltpu.VMEM(lines, F32),
            pltpu.VMEM((2,) + lines, F32),
            pltpu.VMEM(whole, F32),
            pltpu.VMEM((2 * LANES, 2 * LANES), BF16),
            pltpu.VMEM((2 * LANES, 2 * LANES), BF16),
            pltpu.VMEM((3, 2 * LANES, 2 * LANES), BF16),
            pltpu.VMEM((3, 2 * LANES, 2 * LANES), BF16),
            pltpu.VMEM((2 * LANES, targets), BF16),
            pltpu.VMEM((LANES, targets), BF16),
            pltpu.VMEM((CHUNKS, 3, 2, GROUP * block, LANES), F32),
            pltpu.VMEM(first, F32),
            pltpu.VMEM(chunked, F32),
            pltpu.VMEM(chunked, F32),
            pltpu.VMEM(first, F32),
            pltpu.VMEM(chunked, F32),
            pltpu.VMEM(chunked, F32),
            pltpu.VMEM(chunked, F32),
            dma((7,)),
            dma((4,)),
            dma,
            dma((CHUNKS,)),
            dma,
            dma((CHUNKS,)),
            dma,
            dma((CHUNKS,)),
        ],
        compiler_params=pltpu.CompilerParams(
            collective_id=0, has_side_effects=True, vmem_limit_bytes=VMEM_LIMIT
        ),
    )(*[pltpu.with_memory_space_constraint(operand, pltpu.HBM) for operand in operands])
    return result.reshape(1, 1, rows, targets)


def solution(mesh):
    placed = (P("bx", "by", None, None), P("bx", "by", None), P(), P(), P(), P())
    return jax.shard_map(
        shards, mesh=mesh, in_specs=placed, out_specs=P("bx", "by", None, None), check_vma=False
    )
```

```python
import functools
import math

import jax
import jax.numpy as jnp
from jax import lax
from jax.experimental import pallas as pl
from jax.experimental.pallas import tpu as pltpu
from jax.sharding import PartitionSpec as P

MESH = pl.DeviceIdType.MESH
LANES = 128
HALF = 64
GROUP = 8
LEVELS = 4
CHUNKS = 8
Z_FIRST = 2
T_CHUNKS = (5, 7)
X_CHUNKS = (2, 3, 4, 6)
T_LAST = len(T_CHUNKS)
X_COUNT = len(X_CHUNKS)
RETURN_AT = X_COUNT - 1
PEER_ORDER = (6, 4, 7, 3, 5, 1, 2)
VMEM_LIMIT = 32 * 2**20
F32 = jnp.float32
BF16 = jnp.bfloat16


def sine_coefficients(terms):
    import numpy as np

    points = 0.5 * np.cos((np.arange(2000) + 0.5) / 2000 * np.pi / 2)
    basis = np.stack([points ** (2 * k + 1) for k in range(terms)], axis=1)
    solved = np.linalg.lstsq(basis, np.sin(2 * np.pi * points), rcond=None)[0]
    return [float(value) for value in solved]


SINE = sine_coefficients(6)


def split(value):
    high = value.astype(BF16)
    return high, (value - high.astype(F32)).astype(BF16)


def dot(left, right):
    return jnp.dot(left, right, preferred_element_type=F32)


def phase_tables(speed, turns):
    lane = lax.broadcasted_iota(jnp.int32, speed.shape, 1)
    first = lane < HALF
    angle = speed * turns + jnp.where(first, 0.25, 0.0)
    rest = angle - jnp.round(angle)
    square = rest * rest
    total = jnp.full_like(rest, SINE[-1])
    for term in SINE[-2::-1]:
        total = total * square + term
    wave = total * rest
    turned = pltpu.roll(wave, HALF, 1)
    return jnp.where(first, wave, turned), jnp.where(first, -turned, wave)


def rotate(weights, cosine, sine):
    return weights * cosine + pltpu.roll(weights, HALF, 1) * sine


def butterfly_kernel(
    rows, charges_hbm, speed_hbm, omega_hbm, mixers_hbm, source_hbm, target_hbm, out_ref,
    charges, omega, mixers, source, target, speeds, z_speeds, wide_t, source_pair, first_pair, high_mix, low_mix,
    target_pair, target_low, speed_rows, tables, z_raw, z_send, z_recv, a_send, a_back, a_recv, b_send, b_recv,
    t_in, t_out,
    load_sems, speed_sems, send_sems, z_raw_sem, z_recv_sems, a_back_sem, a_recv_sems, b_recv_sems, t_in_sem,
):
    per_peer = rows // GROUP
    block = per_peer // CHUNKS
    half = block // 2
    first_rows = Z_FIRST * block
    last_rows = T_LAST * half
    count = GROUP * block
    x_base, t_base = Z_FIRST * count, (Z_FIRST + X_COUNT) * count
    bx, by = lax.axis_index("bx"), lax.axis_index("by")
    z_count = lax.axis_size("bx") // 2
    y_count = lax.axis_size("by") // 2
    side = lax.rem(bx, 2)
    x_hi, x_lo, core = bx // z_count, by // y_count, lax.rem(by, 2)
    me = x_hi * 4 + core * 2 + x_lo
    across = 1 - 2 * side

    z_peer = {"bx": bx + across}
    peers = []
    cross = []
    for mask in PEER_ORDER:
        other_hi = lax.rem(x_hi + mask // 4, 2)
        other_core = lax.rem(core + mask // 2 % 2, 2)
        other_lo = lax.rem(x_lo + mask % 2, 2)
        to_bx = other_hi * z_count + lax.rem(bx, z_count)
        to_by = other_lo * y_count + (lax.rem(by, y_count) // 2) * 2 + other_core
        place = other_hi * 4 + other_core * 2 + other_lo
        peers.append(({"bx": to_bx, "by": to_by}, place))
        cross.append(({"bx": to_bx + across, "by": to_by}, place))
    cross.append((z_peer, me))

    barrier = pltpu.get_barrier_semaphore()
    for device, _ in cross + peers:
        pl.semaphore_signal(barrier, inc=1, device_id=device, device_id_type=MESH)

    loads = [
        pltpu.make_async_copy(speed_hbm.at[me], speeds.at[side, me], load_sems.at[0]),
        pltpu.make_async_copy(omega_hbm, omega, load_sems.at[1]),
        pltpu.make_async_copy(source_hbm, source, load_sems.at[2]),
        pltpu.make_async_copy(charges_hbm.at[:, pl.ds(0, first_rows)], charges, load_sems.at[3]),
        pltpu.make_async_copy(mixers_hbm, mixers, load_sems.at[4]),
        pltpu.make_async_copy(target_hbm, target, load_sems.at[5]),
        pltpu.make_async_copy(speed_hbm, z_speeds.at[0], load_sems.at[6]),
    ]
    for load in loads:
        load.start()

    def wait_bytes(ref, sem):
        pltpu.make_async_copy(ref, ref, sem).wait()

    def send(source_ref, target_ref, send_sem, recv_sem, device):
        pltpu.make_async_remote_copy(
            src_ref=source_ref, dst_ref=target_ref, send_sem=send_sem, recv_sem=recv_sem,
            device_id=device, device_id_type=MESH,
        ).start()

    def rows_of_chunk(chunk):
        return pl.ds(pl.multiple_of(chunk * block, block), block)

    def half_of(which):
        return pl.ds(pl.multiple_of(which * half, half), half)

    def turns_of(level):
        row = omega[pl.ds(level, 1), :] * (1.0 / (2.0 * math.pi))
        return jnp.concatenate([row, row], axis=1)

    def source_weights(value):
        high, low = split(value)
        both = dot(jnp.concatenate([high, low], axis=1), source_pair[...])
        return both[:, :LANES] + both[:, LANES:]

    def scatter_charges(slot):
        here = rows_of_chunk((T_CHUNKS + X_CHUNKS)[slot])
        for device, place in peers:
            send(charges_hbm.at[place, here], a_recv.at[slot, me], send_sems.at[0], a_recv_sems.at[slot], device)
        pltpu.make_async_copy(charges_hbm.at[me, here], a_recv.at[slot, me], a_recv_sems.at[slot]).start()

    pl.semaphore_wait(barrier, 2 * GROUP - 1)
    send(speed_hbm, z_speeds.at[1], speed_sems.at[0], speed_sems.at[1], z_peer)
    for device, place in peers:
        send(speed_hbm.at[place], speeds.at[side, me], speed_sems.at[2], speed_sems.at[3], device)
    for place in range(GROUP):
        here = pl.ds(0, first_rows)
        send(charges_hbm.at[place, here], z_raw.at[place], send_sems.at[1], z_raw_sem, z_peer)
    scatter_charges(0)

    loads[1].wait()
    loads[2].wait()
    high, low = split(source[...])
    source_pair[0:LANES, 0:LANES] = high
    source_pair[0:LANES, LANES:] = low
    source_pair[LANES:, 0:LANES] = high
    source_pair[LANES:, LANES:] = jnp.zeros_like(high)

    loads[4].wait()
    for child in range(2):
        span = slice(child * LANES, (child + 1) * LANES)
        high, low = split(mixers[0, side, lax.rem(side + child, 2)])
        first_pair[span, 0:LANES] = high
        first_pair[span, LANES:] = low
        for level in range(LEVELS):
            for target_half in range(2):
                high, low = split(mixers[level, target_half, child])
                place = (level, span, slice(target_half * LANES, (target_half + 1) * LANES))
                high_mix[place] = high
                low_mix[place] = low

    scatter_charges(1)

    loads[5].wait()
    high, low = split(target[...])
    target_pair[0:LANES, :] = high
    target_pair[LANES:, :] = high
    target_low[...] = low
    scatter_charges(2)

    def t_forward(index):
        here = pl.ds(index * half, half)
        wait_bytes(a_recv.at[index], a_recv_sems.at[index])
        for place in range(GROUP):
            send(
                a_recv.at[index, place, half_of(1 - side)], t_in.at[side, place, here],
                send_sems.at[2], t_in_sem, z_peer,
            )
        t_in[side, :, here, :] = a_recv[index, :, half_of(side), :]

    t_forward(0)
    loads[0].wait()
    wait_bytes(speeds.at[0, pl.ds(0, GROUP - 1)], speed_sems.at[3])
    send(speeds.at[side], speeds.at[side], speed_sems.at[4], speed_sems.at[5], z_peer)
    scatter_charges(3)

    def widen(into, columns):
        for place in range(GROUP):
            into[place] = jnp.broadcast_to(columns[:, place:place + 1], (columns.shape[0], LANES))

    groups = per_peer // LANES
    for group in range(groups):
        columns = jnp.transpose(speeds[side, :, group, :])
        for place in range(GROUP):
            if group == 0:
                speed_rows[place * first_rows:(place + 1) * first_rows] = jnp.broadcast_to(
                    columns[:first_rows, place:place + 1], (first_rows, LANES)
                )
            for index, chunk in enumerate(X_CHUNKS):
                start = chunk * block - group * LANES
                into = x_base + index * count + place * block
                if 0 <= start < LANES:
                    speed_rows[into:into + block] = jnp.broadcast_to(
                        columns[start:start + block, place:place + 1], (block, LANES)
                    )

    def fill_tables(first, blocks, levels):
        def body(index, carry):
            here = pl.ds(pl.multiple_of(first + index * count, count), count)
            for level in levels:
                cosine, sine = phase_tables(speed_rows[here, :], turns_of(level))
                tables[level, 0, here, :] = cosine
                tables[level, 1, here, :] = sine
            return carry

        lax.fori_loop(0, blocks, body, 0)

    for slot in range(4, T_LAST + X_COUNT):
        scatter_charges(slot)
    fill_tables(x_base, X_COUNT, range(LEVELS))
    for index in range(1, T_LAST):
        t_forward(index)
    fill_tables(0, Z_FIRST, range(1, LEVELS))

    def mix(rotated, level, stride, size):
        places = rotated.shape[0] // size
        low_places = [place for place in range(places) if place // stride % 2 == 0]

        def gather(shift):
            parts = [rotated[(place + shift) * size:(place + shift + 1) * size] for place in low_places]
            return jnp.concatenate(parts, axis=0)

        high, low = split(jnp.concatenate([gather(0), gather(stride)], axis=1))
        both = dot(jnp.concatenate([high, low], axis=0), high_mix[level])
        count = high.shape[0]
        mixed = both[:count] + both[count:] + dot(high, low_mix[level])
        parts = [None] * places
        for index, place in enumerate(low_places):
            taken = mixed[index * size:(index + 1) * size]
            parts[place] = taken[:, :LANES]
            parts[place + stride] = taken[:, LANES:]
        return jnp.concatenate(parts, axis=0)

    def turned(weights, level, here):
        return rotate(weights, tables[level, 0, here, :], tables[level, 1, here, :])

    def other_levels(weights, here, size):
        for level in range(1, LEVELS):
            weights = mix(turned(weights, level, here), level, {1: 4, 2: 2, 3: 1}[level], size)
        return weights

    def first_level(own, other):
        high, low = split(jnp.concatenate([own, other], axis=1))
        both = dot(high, first_pair[...])
        return both[:, :LANES] + both[:, LANES:] + dot(low, first_pair[:, :LANES])

    def x_rows(index):
        return pl.ds(pl.multiple_of(x_base + index * count, count), count)

    def x_first_start(index, carry):
        slot = index + T_LAST
        wait_bytes(a_recv.at[slot], a_recv_sems.at[slot])
        weights = source_weights(a_recv[slot].reshape(count, LANES))
        z_send[index] = turned(weights, 0, x_rows(index)).reshape(GROUP, block, LANES)
        for place in range(GROUP):
            send(z_send.at[index, place], z_recv.at[index, place], send_sems.at[3], z_recv_sems.at[index], z_peer)
        return carry

    def give_back(slot, chunk):
        for device, place in peers:
            send(b_send.at[slot, place], b_recv.at[chunk, me], send_sems.at[4], b_recv_sems.at[chunk], device)
        pltpu.make_async_copy(b_send.at[slot, me], b_recv.at[chunk, me], b_recv_sems.at[chunk]).start()

    def x_first_end(index, carry):
        @pl.when(index == RETURN_AT)
        def _():
            for piece in range(T_LAST):
                t_back(piece, 1 - side, cross, send_sems.at[7])

        wait_bytes(z_recv.at[index], z_recv_sems.at[index])
        weights = first_level(z_send[index].reshape(count, LANES), z_recv[index].reshape(count, LANES))
        weights = other_levels(weights, x_rows(index), block)
        slot = Z_FIRST + index
        b_send[slot] = weights.reshape(GROUP, block, LANES)
        give_back(slot, slot + (X_CHUNKS[-1] - X_CHUNKS[-2] - 1) * (index // (X_COUNT - 1)))
        return carry

    def targets(chunk, carry):
        wait_bytes(b_recv.at[chunk], b_recv_sems.at[chunk])
        high, low = split(b_recv[chunk].reshape(GROUP * block, LANES))
        both = jnp.concatenate([high, low], axis=1)
        width = 2 * LANES
        for column in range(0, out_ref.shape[2], width):
            here = slice(column, column + width)
            total = dot(both, target_pair[:, here]) + dot(high, target_low[:, here])
            out_ref[:, rows_of_chunk(chunk), here] = total.astype(BF16).reshape(GROUP, block, width)
        return carry

    loads[3].wait()
    loads[6].wait()
    wait_bytes(z_speeds.at[1], speed_sems.at[1])
    wait_bytes(z_raw, z_raw_sem)
    first_count = GROUP * first_rows
    sides = []
    for index, value in enumerate((charges, z_raw)):
        columns = jnp.transpose(z_speeds[index, :, 0, :])
        speed_here = jnp.concatenate(
            [
                jnp.broadcast_to(columns[:first_rows, place:place + 1], (first_rows, LANES))
                for place in range(GROUP)
            ],
            axis=0,
        )
        cosine, sine = phase_tables(speed_here, turns_of(0))
        sides.append(rotate(source_weights(value[...].reshape(first_count, LANES)), cosine, sine))
    a_send[...] = first_level(*sides).reshape(GROUP, first_rows, LANES)
    for device, place in peers:
        send(a_send.at[place], a_back.at[me], send_sems.at[5], a_back_sem, device)
    pltpu.make_async_copy(a_send.at[me], a_back.at[me], a_back_sem).start()

    x_first_start(0, 0)

    wait_bytes(speeds.at[0], speed_sems.at[5])
    for plane in range(2):
        columns = jnp.transpose(speeds[plane, :, groups - 1, :])
        widen(wide_t.at[plane], columns)
    for plane in range(2):
        for place in range(GROUP):
            for piece, chunk in enumerate(T_CHUNKS):
                start = pl.multiple_of(chunk * block - (groups - 1) * LANES + side * half, half)
                into = t_base + (plane * GROUP + place) * last_rows + piece * half
                speed_rows[into:into + half] = wide_t[plane, place, pl.ds(start, half), :]
    fill_tables(t_base, T_LAST, range(LEVELS))
    lax.fori_loop(1, X_COUNT, x_first_start, 0)
    wait_bytes(t_in.at[0], t_in_sem)
    weights = source_weights(t_in[...].reshape(2 * GROUP * last_rows, LANES))
    t_rows = slice(t_base, t_base + 2 * GROUP * last_rows)
    weights = mix(turned(weights, 0, t_rows), 0, GROUP, last_rows)
    weights = other_levels(weights, t_rows, last_rows)
    t_out[...] = weights.reshape(2, GROUP, last_rows, LANES)

    def t_back(index, plane, devices, sem):
        chunk = T_CHUNKS[index]
        here = pl.ds(index * half, half)
        for device, place in devices:
            send(
                t_out.at[plane, place, here], b_recv.at[chunk, me, half_of(side)],
                sem, b_recv_sems.at[chunk], device,
            )

    for index in range(T_LAST):
        t_back(index, side, peers, send_sems.at[6])
        pltpu.make_async_copy(
            t_out.at[side, me, pl.ds(index * half, half)],
            b_recv.at[T_CHUNKS[index], me, half_of(side)],
            b_recv_sems.at[T_CHUNKS[index]],
        ).start()

    wait_bytes(a_back, a_back_sem)
    weights = other_levels(a_back[...].reshape(first_count, LANES), slice(0, x_base), first_rows)
    for chunk in range(Z_FIRST):
        b_send[chunk] = weights.reshape(GROUP, first_rows, LANES)[:, chunk * block:(chunk + 1) * block, :]
        give_back(chunk, chunk)

    lax.fori_loop(0, X_COUNT, x_first_end, 0)
    lax.fori_loop(0, CHUNKS, targets, 0)

    most = pl.ds(0, GROUP - 1)
    wait_bytes(a_recv.at[:, most], send_sems.at[0])
    wait_bytes(z_raw, send_sems.at[1])
    wait_bytes(t_in.at[0], send_sems.at[2])
    wait_bytes(z_recv, send_sems.at[3])
    wait_bytes(b_send.at[:, most], send_sems.at[4])
    wait_bytes(a_back.at[most], send_sems.at[5])
    wait_bytes(t_in.at[0, most], send_sems.at[6])
    wait_bytes(t_in.at[0], send_sems.at[7])
    wait_bytes(z_speeds.at[1], speed_sems.at[0])
    wait_bytes(speeds.at[0, most], speed_sems.at[2])
    wait_bytes(speeds.at[0], speed_sems.at[4])


def shards(charges, speed, omega, mixers, source_map, target_map):
    rows, targets = charges.shape[2], target_map.shape[1]
    per_peer = rows // GROUP
    block = per_peer // CHUNKS
    first_rows, last_rows = Z_FIRST * block, T_LAST * block // 2
    whole = (GROUP, per_peer, LANES)
    lines = (GROUP, per_peer // LANES, LANES)
    square = (2 * LANES, 2 * LANES)
    dma = pltpu.SemaphoreType.DMA
    operands = [charges.reshape(whole), speed.reshape(lines), omega, mixers, source_map, target_map]
    result = pl.pallas_call(
        functools.partial(butterfly_kernel, rows),
        name="butterfly",
        out_shape=pltpu.VMEM((GROUP, per_peer, targets), BF16),
        in_specs=[pl.BlockSpec(memory_space=pltpu.HBM)] * len(operands),
        out_specs=pl.BlockSpec(memory_space=pltpu.VMEM),
        scratch_shapes=[
            pltpu.VMEM((GROUP, first_rows, LANES), F32),
            pltpu.VMEM((LEVELS, HALF), F32),
            pltpu.VMEM((LEVELS, 2, 2, LANES, LANES), F32),
            pltpu.VMEM((LANES, LANES), F32),
            pltpu.VMEM((LANES, targets), F32),
            pltpu.VMEM((2,) + lines, F32),
            pltpu.VMEM((2,) + lines, F32),
            pltpu.VMEM((2, GROUP, LANES, LANES), F32),
            pltpu.VMEM(square, BF16),
            pltpu.VMEM(square, BF16),
            pltpu.VMEM((LEVELS,) + square, BF16),
            pltpu.VMEM((LEVELS,) + square, BF16),
            pltpu.VMEM((2 * LANES, targets), BF16),
            pltpu.VMEM((LANES, targets), BF16),
            pltpu.VMEM((rows, LANES), F32),
            pltpu.VMEM((LEVELS, 2, rows, LANES), F32),
            pltpu.VMEM((GROUP, first_rows, LANES), F32),
            pltpu.VMEM((X_COUNT, GROUP, block, LANES), F32),
            pltpu.VMEM((X_COUNT, GROUP, block, LANES), F32),
            pltpu.VMEM((GROUP, first_rows, LANES), F32),
            pltpu.VMEM((GROUP, first_rows, LANES), F32),
            pltpu.VMEM((CHUNKS - Z_FIRST, GROUP, block, LANES), F32),
            pltpu.VMEM((CHUNKS - T_LAST, GROUP, block, LANES), F32),
            pltpu.VMEM((CHUNKS, GROUP, block, LANES), F32),
            pltpu.VMEM((2, GROUP, last_rows, LANES), F32),
            pltpu.VMEM((2, GROUP, last_rows, LANES), F32),
            dma((7,)),
            dma((6,)),
            dma((8,)),
            dma,
            dma((X_COUNT,)),
            dma,
            dma((CHUNKS - Z_FIRST,)),
            dma((CHUNKS,)),
            dma,
        ],
        compiler_params=pltpu.CompilerParams(
            collective_id=0, has_side_effects=True, vmem_limit_bytes=VMEM_LIMIT
        ),
    )(*[pltpu.with_memory_space_constraint(operand, pltpu.HBM) for operand in operands])
    return result.reshape(1, 1, rows, targets)


def solution(mesh):
    placed = (P("bx", "by", None, None), P("bx", "by", None), P(), P(), P(), P())
    return jax.shard_map(
        shards, mesh=mesh, in_specs=placed, out_specs=P("bx", "by", None, None), check_vma=False
    )
```

```python
import functools
import math

import jax
import jax.numpy as jnp
from jax import lax
from jax.experimental import pallas as pl
from jax.experimental.pallas import tpu as pltpu
from jax.sharding import PartitionSpec as P

MESH = pl.DeviceIdType.MESH
LANES = 128
HALF = 64
GROUP = 8
LEVELS = 4
CHUNKS = 8
Z_FIRST = 2
T_CHUNKS = (5, 7)
X_CHUNKS = (2, 3, 4, 6)
T_LAST = len(T_CHUNKS)
X_COUNT = len(X_CHUNKS)
RETURN_AT = X_COUNT - 1
HERE = 4
PEER_ORDER = (4, 5, 1, 6, 7, 3, 2)
VMEM_LIMIT = 32 * 2**20
F32 = jnp.float32
BF16 = jnp.bfloat16


def sine_coefficients(terms):
    import numpy as np

    points = 0.5 * np.cos((np.arange(2000) + 0.5) / 2000 * np.pi / 2)
    basis = np.stack([points ** (2 * k + 1) for k in range(terms)], axis=1)
    solved = np.linalg.lstsq(basis, np.sin(2 * np.pi * points), rcond=None)[0]
    return [float(value) for value in solved]


SINE = sine_coefficients(6)


def split(value):
    high = value.astype(BF16)
    return high, (value - high.astype(F32)).astype(BF16)


def dot(left, right):
    return jnp.dot(left, right, preferred_element_type=F32)


def phase_tables(speed, turns):
    lane = lax.broadcasted_iota(jnp.int32, speed.shape, 1)
    first = lane < HALF
    angle = speed * turns + jnp.where(first, 0.25, 0.0)
    rest = angle - jnp.round(angle)
    square = rest * rest
    total = jnp.full_like(rest, SINE[-1])
    for term in SINE[-2::-1]:
        total = total * square + term
    wave = total * rest
    turned = pltpu.roll(wave, HALF, 1)
    return jnp.where(first, wave, turned), jnp.where(first, -turned, wave)


def rotate(weights, cosine, sine):
    return weights * cosine + pltpu.roll(weights, HALF, 1) * sine


def map_chunk(weights_ref, pair_ref, low_ref, into_ref):
    places, block, _ = weights_ref.shape
    high, low = split(weights_ref[...].reshape(places * block, LANES))
    both = jnp.concatenate([high, low], axis=1)
    width = 2 * LANES
    for column in range(0, pair_ref.shape[1], width):
        here = slice(column, column + width)
        total = dot(both, pair_ref[:, here]) + dot(high, low_ref[:, here])
        into_ref[:, :, here] = total.astype(BF16).reshape(places, block, width)


def last_kernel(done, weights, pair, low, out_hbm, rest, sems):
    ready = done.shape[1]
    block = weights.shape[2]
    copies = [
        pltpu.make_async_copy(done.at[place], out_hbm.at[place, pl.ds(0, ready)], sems.at[place])
        for place in range(GROUP)
    ]
    for copy in copies:
        copy.start()
    for index in range(CHUNKS - HERE):
        map_chunk(weights.at[HERE + index], pair, low, rest.at[index])
        copy = pltpu.make_async_copy(
            rest.at[index], out_hbm.at[:, pl.ds(ready + index * block, block)], sems.at[GROUP + index]
        )
        copy.start()
        copies.append(copy)
    for copy in copies:
        copy.wait()


def butterfly_kernel(
    rows, charges_hbm, speed_hbm, omega_hbm, mixers_hbm, source_hbm, target_hbm,
    out_ref, b_recv, target_pair, target_low,
    charges, omega, mixers, source, target, speeds, z_speeds, wide_t, source_pair, first_pair, high_mix, low_mix,
    speed_rows, tables, z_raw, z_send, z_recv, a_send, a_back, a_recv, b_send,
    t_in, t_out,
    load_sems, speed_sems, send_sems, z_raw_sem, z_recv_sems, a_back_sem, a_recv_sems, b_recv_sems, t_in_sem,
):
    per_peer = rows // GROUP
    block = per_peer // CHUNKS
    half = block // 2
    first_rows = Z_FIRST * block
    last_rows = T_LAST * half
    count = GROUP * block
    x_base, t_base = Z_FIRST * count, (Z_FIRST + X_COUNT) * count
    bx, by = lax.axis_index("bx"), lax.axis_index("by")
    z_count = lax.axis_size("bx") // 2
    y_count = lax.axis_size("by") // 2
    side = lax.rem(bx, 2)
    x_hi, x_lo, core = bx // z_count, by // y_count, lax.rem(by, 2)
    me = x_hi * 4 + core * 2 + x_lo
    across = 1 - 2 * side

    z_peer = {"bx": bx + across}
    peers = []
    cross = []
    for mask in PEER_ORDER:
        other_hi = lax.rem(x_hi + mask // 4, 2)
        other_core = lax.rem(core + mask // 2 % 2, 2)
        other_lo = lax.rem(x_lo + mask % 2, 2)
        to_bx = other_hi * z_count + lax.rem(bx, z_count)
        to_by = other_lo * y_count + (lax.rem(by, y_count) // 2) * 2 + other_core
        place = other_hi * 4 + other_core * 2 + other_lo
        peers.append(({"bx": to_bx, "by": to_by}, place))
        cross.append(({"bx": to_bx + across, "by": to_by}, place))
    cross.append((z_peer, me))

    barrier = pltpu.get_barrier_semaphore()
    for device, _ in cross + peers:
        pl.semaphore_signal(barrier, inc=1, device_id=device, device_id_type=MESH)

    loads = [
        pltpu.make_async_copy(speed_hbm.at[me], speeds.at[side, me], load_sems.at[0]),
        pltpu.make_async_copy(omega_hbm, omega, load_sems.at[1]),
        pltpu.make_async_copy(source_hbm, source, load_sems.at[2]),
        pltpu.make_async_copy(charges_hbm.at[:, pl.ds(0, first_rows)], charges, load_sems.at[3]),
        pltpu.make_async_copy(mixers_hbm, mixers, load_sems.at[4]),
        pltpu.make_async_copy(target_hbm, target, load_sems.at[5]),
        pltpu.make_async_copy(speed_hbm, z_speeds.at[0], load_sems.at[6]),
    ]
    for load in loads:
        load.start()

    def wait_bytes(ref, sem):
        pltpu.make_async_copy(ref, ref, sem).wait()

    def send(source_ref, target_ref, send_sem, recv_sem, device):
        pltpu.make_async_remote_copy(
            src_ref=source_ref, dst_ref=target_ref, send_sem=send_sem, recv_sem=recv_sem,
            device_id=device, device_id_type=MESH,
        ).start()

    def rows_of_chunk(chunk):
        return pl.ds(pl.multiple_of(chunk * block, block), block)

    def half_of(which):
        return pl.ds(pl.multiple_of(which * half, half), half)

    def turns_of(level):
        row = omega[pl.ds(level, 1), :] * (1.0 / (2.0 * math.pi))
        return jnp.concatenate([row, row], axis=1)

    def source_weights(value):
        high, low = split(value)
        both = dot(jnp.concatenate([high, low], axis=1), source_pair[...])
        return both[:, :LANES] + both[:, LANES:]

    def scatter_charges(slot):
        here = rows_of_chunk((T_CHUNKS + X_CHUNKS)[slot])
        for device, place in peers:
            send(charges_hbm.at[place, here], a_recv.at[slot, me], send_sems.at[0], a_recv_sems.at[slot], device)
        pltpu.make_async_copy(charges_hbm.at[me, here], a_recv.at[slot, me], a_recv_sems.at[slot]).start()

    pl.semaphore_wait(barrier, 2 * GROUP - 1)
    send(speed_hbm, z_speeds.at[1], speed_sems.at[0], speed_sems.at[1], z_peer)
    for device, place in peers:
        send(speed_hbm.at[place], speeds.at[side, me], speed_sems.at[2], speed_sems.at[3], device)
    for place in range(GROUP):
        here = pl.ds(0, first_rows)
        send(charges_hbm.at[place, here], z_raw.at[place], send_sems.at[1], z_raw_sem, z_peer)
    scatter_charges(0)

    loads[1].wait()
    loads[2].wait()
    high, low = split(source[...])
    source_pair[0:LANES, 0:LANES] = high
    source_pair[0:LANES, LANES:] = low
    source_pair[LANES:, 0:LANES] = high
    source_pair[LANES:, LANES:] = jnp.zeros_like(high)

    loads[4].wait()
    for child in range(2):
        span = slice(child * LANES, (child + 1) * LANES)
        high, low = split(mixers[0, side, lax.rem(side + child, 2)])
        first_pair[span, 0:LANES] = high
        first_pair[span, LANES:] = low
        for level in range(LEVELS):
            for target_half in range(2):
                high, low = split(mixers[level, target_half, child])
                place = (level, span, slice(target_half * LANES, (target_half + 1) * LANES))
                high_mix[place] = high
                low_mix[place] = low

    scatter_charges(1)

    loads[5].wait()
    high, low = split(target[...])
    target_pair[0:LANES, :] = high
    target_pair[LANES:, :] = high
    target_low[...] = low
    scatter_charges(2)

    def t_forward(index):
        here = pl.ds(index * half, half)
        wait_bytes(a_recv.at[index], a_recv_sems.at[index])
        for place in range(GROUP):
            send(
                a_recv.at[index, place, half_of(1 - side)], t_in.at[side, place, here],
                send_sems.at[2], t_in_sem, z_peer,
            )
        t_in[side, :, here, :] = a_recv[index, :, half_of(side), :]

    t_forward(0)
    loads[0].wait()
    wait_bytes(speeds.at[0, pl.ds(0, GROUP - 1)], speed_sems.at[3])
    send(speeds.at[side], speeds.at[side], speed_sems.at[4], speed_sems.at[5], z_peer)
    scatter_charges(3)

    def widen(into, columns):
        for place in range(GROUP):
            into[place] = jnp.broadcast_to(columns[:, place:place + 1], (columns.shape[0], LANES))

    groups = per_peer // LANES
    for group in range(groups):
        columns = jnp.transpose(speeds[side, :, group, :])
        for place in range(GROUP):
            if group == 0:
                speed_rows[place * first_rows:(place + 1) * first_rows] = jnp.broadcast_to(
                    columns[:first_rows, place:place + 1], (first_rows, LANES)
                )
            for index, chunk in enumerate(X_CHUNKS):
                start = chunk * block - group * LANES
                into = x_base + index * count + place * block
                if 0 <= start < LANES:
                    speed_rows[into:into + block] = jnp.broadcast_to(
                        columns[start:start + block, place:place + 1], (block, LANES)
                    )

    def fill_tables(first, blocks, levels):
        def body(index, carry):
            here = pl.ds(pl.multiple_of(first + index * count, count), count)
            for level in levels:
                cosine, sine = phase_tables(speed_rows[here, :], turns_of(level))
                tables[level, 0, here, :] = cosine
                tables[level, 1, here, :] = sine
            return carry

        lax.fori_loop(0, blocks, body, 0)

    for slot in range(4, T_LAST + X_COUNT):
        scatter_charges(slot)
    fill_tables(x_base, X_COUNT, range(LEVELS))
    for index in range(1, T_LAST):
        t_forward(index)
    fill_tables(0, Z_FIRST, range(1, LEVELS))

    def mix(rotated, level, stride, size):
        places = rotated.shape[0] // size
        low_places = [place for place in range(places) if place // stride % 2 == 0]

        def gather(shift):
            parts = [rotated[(place + shift) * size:(place + shift + 1) * size] for place in low_places]
            return jnp.concatenate(parts, axis=0)

        high, low = split(jnp.concatenate([gather(0), gather(stride)], axis=1))
        both = dot(jnp.concatenate([high, low], axis=0), high_mix[level])
        count = high.shape[0]
        mixed = both[:count] + both[count:] + dot(high, low_mix[level])
        parts = [None] * places
        for index, place in enumerate(low_places):
            taken = mixed[index * size:(index + 1) * size]
            parts[place] = taken[:, :LANES]
            parts[place + stride] = taken[:, LANES:]
        return jnp.concatenate(parts, axis=0)

    def turned(weights, level, here):
        return rotate(weights, tables[level, 0, here, :], tables[level, 1, here, :])

    def other_levels(weights, here, size):
        for level in range(1, LEVELS):
            weights = mix(turned(weights, level, here), level, {1: 4, 2: 2, 3: 1}[level], size)
        return weights

    def first_level(own, other):
        high, low = split(jnp.concatenate([own, other], axis=1))
        both = dot(high, first_pair[...])
        return both[:, :LANES] + both[:, LANES:] + dot(low, first_pair[:, :LANES])

    def x_rows(index):
        return pl.ds(pl.multiple_of(x_base + index * count, count), count)

    def x_first_start(index, carry):
        slot = index + T_LAST
        wait_bytes(a_recv.at[slot], a_recv_sems.at[slot])
        weights = source_weights(a_recv[slot].reshape(count, LANES))
        z_send[index] = turned(weights, 0, x_rows(index)).reshape(GROUP, block, LANES)
        for place in range(GROUP):
            send(z_send.at[index, place], z_recv.at[index, place], send_sems.at[3], z_recv_sems.at[index], z_peer)
        return carry

    def give_back(slot, chunk):
        for device, place in peers:
            send(b_send.at[slot, place], b_recv.at[chunk, me], send_sems.at[4], b_recv_sems.at[chunk], device)
        pltpu.make_async_copy(b_send.at[slot, me], b_recv.at[chunk, me], b_recv_sems.at[chunk]).start()

    def x_first_end(index, carry):
        @pl.when(index == RETURN_AT)
        def _():
            for piece in range(T_LAST):
                t_back(piece, 1 - side, cross, send_sems.at[7])

        wait_bytes(z_recv.at[index], z_recv_sems.at[index])
        weights = first_level(z_send[index].reshape(count, LANES), z_recv[index].reshape(count, LANES))
        weights = other_levels(weights, x_rows(index), block)
        slot = Z_FIRST + index
        b_send[slot] = weights.reshape(GROUP, block, LANES)
        give_back(slot, slot + (X_CHUNKS[-1] - X_CHUNKS[-2] - 1) * (index // (X_COUNT - 1)))
        return carry

    def targets(chunk, carry):
        wait_bytes(b_recv.at[chunk], b_recv_sems.at[chunk])
        map_chunk(b_recv.at[chunk], target_pair, target_low, out_ref.at[:, rows_of_chunk(chunk), :])
        return carry

    loads[3].wait()
    loads[6].wait()
    wait_bytes(z_speeds.at[1], speed_sems.at[1])
    wait_bytes(z_raw, z_raw_sem)
    first_count = GROUP * first_rows
    sides = []
    for index, value in enumerate((charges, z_raw)):
        columns = jnp.transpose(z_speeds[index, :, 0, :])
        speed_here = jnp.concatenate(
            [
                jnp.broadcast_to(columns[:first_rows, place:place + 1], (first_rows, LANES))
                for place in range(GROUP)
            ],
            axis=0,
        )
        cosine, sine = phase_tables(speed_here, turns_of(0))
        sides.append(rotate(source_weights(value[...].reshape(first_count, LANES)), cosine, sine))
    a_send[...] = first_level(*sides).reshape(GROUP, first_rows, LANES)
    for device, place in peers:
        send(a_send.at[place], a_back.at[me], send_sems.at[5], a_back_sem, device)
    pltpu.make_async_copy(a_send.at[me], a_back.at[me], a_back_sem).start()

    x_first_start(0, 0)

    wait_bytes(speeds.at[0], speed_sems.at[5])
    for plane in range(2):
        columns = jnp.transpose(speeds[plane, :, groups - 1, :])
        widen(wide_t.at[plane], columns)
    for plane in range(2):
        for place in range(GROUP):
            for piece, chunk in enumerate(T_CHUNKS):
                start = pl.multiple_of(chunk * block - (groups - 1) * LANES + side * half, half)
                into = t_base + (plane * GROUP + place) * last_rows + piece * half
                speed_rows[into:into + half] = wide_t[plane, place, pl.ds(start, half), :]
    fill_tables(t_base, T_LAST, range(LEVELS))
    lax.fori_loop(1, X_COUNT, x_first_start, 0)
    wait_bytes(t_in.at[0], t_in_sem)
    weights = source_weights(t_in[...].reshape(2 * GROUP * last_rows, LANES))
    t_rows = slice(t_base, t_base + 2 * GROUP * last_rows)
    weights = mix(turned(weights, 0, t_rows), 0, GROUP, last_rows)
    weights = other_levels(weights, t_rows, last_rows)
    t_out[...] = weights.reshape(2, GROUP, last_rows, LANES)

    def t_back(index, plane, devices, sem):
        chunk = T_CHUNKS[index]
        here = pl.ds(index * half, half)
        for device, place in devices:
            send(
                t_out.at[plane, place, here], b_recv.at[chunk, me, half_of(side)],
                sem, b_recv_sems.at[chunk], device,
            )

    for index in range(T_LAST):
        t_back(index, side, peers, send_sems.at[6])
        pltpu.make_async_copy(
            t_out.at[side, me, pl.ds(index * half, half)],
            b_recv.at[T_CHUNKS[index], me, half_of(side)],
            b_recv_sems.at[T_CHUNKS[index]],
        ).start()

    wait_bytes(a_back, a_back_sem)
    weights = other_levels(a_back[...].reshape(first_count, LANES), slice(0, x_base), first_rows)
    for chunk in range(Z_FIRST):
        b_send[chunk] = weights.reshape(GROUP, first_rows, LANES)[:, chunk * block:(chunk + 1) * block, :]
        give_back(chunk, chunk)

    lax.fori_loop(0, X_COUNT, x_first_end, 0)
    lax.fori_loop(0, HERE, targets, 0)
    for chunk in range(HERE, CHUNKS):
        wait_bytes(b_recv.at[chunk], b_recv_sems.at[chunk])

    most = pl.ds(0, GROUP - 1)
    wait_bytes(a_recv.at[:, most], send_sems.at[0])
    wait_bytes(z_raw, send_sems.at[1])
    wait_bytes(t_in.at[0], send_sems.at[2])
    wait_bytes(z_recv, send_sems.at[3])
    wait_bytes(b_send.at[:, most], send_sems.at[4])
    wait_bytes(a_back.at[most], send_sems.at[5])
    wait_bytes(t_in.at[0, most], send_sems.at[6])
    wait_bytes(t_in.at[0], send_sems.at[7])
    wait_bytes(z_speeds.at[1], speed_sems.at[0])
    wait_bytes(speeds.at[0, most], speed_sems.at[2])
    wait_bytes(speeds.at[0], speed_sems.at[4])


def shards(charges, speed, omega, mixers, source_map, target_map):
    rows, targets = charges.shape[2], target_map.shape[1]
    per_peer = rows // GROUP
    block = per_peer // CHUNKS
    first_rows, last_rows = Z_FIRST * block, T_LAST * block // 2
    whole = (GROUP, per_peer, LANES)
    lines = (GROUP, per_peer // LANES, LANES)
    square = (2 * LANES, 2 * LANES)
    dma = pltpu.SemaphoreType.DMA
    operands = [charges.reshape(whole), speed.reshape(lines), omega, mixers, source_map, target_map]
    done, weights, pair, low = pl.pallas_call(
        functools.partial(butterfly_kernel, rows),
        name="butterfly",
        out_shape=(
            pltpu.VMEM((GROUP, HERE * block, targets), BF16),
            pltpu.VMEM((CHUNKS, GROUP, block, LANES), F32),
            pltpu.VMEM((2 * LANES, targets), BF16),
            pltpu.VMEM((LANES, targets), BF16),
        ),
        in_specs=[pl.BlockSpec(memory_space=pltpu.HBM)] * len(operands),
        out_specs=(pl.BlockSpec(memory_space=pltpu.VMEM),) * 4,
        scratch_shapes=[
            pltpu.VMEM((GROUP, first_rows, LANES), F32),
            pltpu.VMEM((LEVELS, HALF), F32),
            pltpu.VMEM((LEVELS, 2, 2, LANES, LANES), F32),
            pltpu.VMEM((LANES, LANES), F32),
            pltpu.VMEM((LANES, targets), F32),
            pltpu.VMEM((2,) + lines, F32),
            pltpu.VMEM((2,) + lines, F32),
            pltpu.VMEM((2, GROUP, LANES, LANES), F32),
            pltpu.VMEM(square, BF16),
            pltpu.VMEM(square, BF16),
            pltpu.VMEM((LEVELS,) + square, BF16),
            pltpu.VMEM((LEVELS,) + square, BF16),
            pltpu.VMEM((rows, LANES), F32),
            pltpu.VMEM((LEVELS, 2, rows, LANES), F32),
            pltpu.VMEM((GROUP, first_rows, LANES), F32),
            pltpu.VMEM((X_COUNT, GROUP, block, LANES), F32),
            pltpu.VMEM((X_COUNT, GROUP, block, LANES), F32),
            pltpu.VMEM((GROUP, first_rows, LANES), F32),
            pltpu.VMEM((GROUP, first_rows, LANES), F32),
            pltpu.VMEM((CHUNKS - Z_FIRST, GROUP, block, LANES), F32),
            pltpu.VMEM((CHUNKS - T_LAST, GROUP, block, LANES), F32),
            pltpu.VMEM((2, GROUP, last_rows, LANES), F32),
            pltpu.VMEM((2, GROUP, last_rows, LANES), F32),
            dma((7,)),
            dma((6,)),
            dma((8,)),
            dma,
            dma((X_COUNT,)),
            dma,
            dma((CHUNKS - Z_FIRST,)),
            dma((CHUNKS,)),
            dma,
        ],
        compiler_params=pltpu.CompilerParams(
            collective_id=0, has_side_effects=True, vmem_limit_bytes=VMEM_LIMIT
        ),
    )(*[pltpu.with_memory_space_constraint(operand, pltpu.HBM) for operand in operands])
    parts = [pltpu.with_memory_space_constraint(part, pltpu.VMEM) for part in (done, weights, pair, low)]
    result = pl.pallas_call(
        last_kernel,
        name="last",
        out_shape=jax.ShapeDtypeStruct((GROUP, per_peer, targets), BF16),
        in_specs=[pl.BlockSpec(memory_space=pltpu.VMEM)] * 4,
        out_specs=pl.BlockSpec(memory_space=pl.ANY),
        scratch_shapes=[pltpu.VMEM((CHUNKS - HERE, GROUP, block, targets), BF16), dma((GROUP + CHUNKS - HERE,))],
        compiler_params=pltpu.CompilerParams(vmem_limit_bytes=8 * 2**20),
    )(*parts)
    return result.reshape(1, 1, rows, targets)


def solution(mesh):
    placed = (P("bx", "by", None, None), P("bx", "by", None), P(), P(), P(), P())
    return jax.shard_map(
        shards, mesh=mesh, in_specs=placed, out_specs=P("bx", "by", None, None), check_vma=False
    )
```

```python
import functools
import math

import jax
import jax.numpy as jnp
from jax import lax
from jax.experimental import pallas as pl
from jax.experimental.pallas import tpu as pltpu
from jax.sharding import PartitionSpec as P

MESH = pl.DeviceIdType.MESH
LANES = 128
HALF = 64
GROUP = 8
LEVELS = 4
CHUNKS = 8
Z_FIRST = 2
T_CHUNKS = (5, 7)
X_CHUNKS = (2, 3, 4, 6)
T_LAST = len(T_CHUNKS)
X_COUNT = len(X_CHUNKS)
RETURN_AT = X_COUNT - 1
HERE = 4
PEER_ORDER = (4, 5, 1, 6, 7, 3, 2)
VMEM_LIMIT = 32 * 2**20
F32 = jnp.float32
BF16 = jnp.bfloat16


def sine_coefficients(terms):
    import numpy as np

    points = 0.5 * np.cos((np.arange(2000) + 0.5) / 2000 * np.pi / 2)
    basis = np.stack([points ** (2 * k + 1) for k in range(terms)], axis=1)
    solved = np.linalg.lstsq(basis, np.sin(2 * np.pi * points), rcond=None)[0]
    return [float(value) for value in solved]


SINE = sine_coefficients(6)


def split(value):
    high = value.astype(BF16)
    return high, (value - high.astype(F32)).astype(BF16)


def dot(left, right):
    return jnp.dot(left, right, preferred_element_type=F32)


def phase_tables(speed, turns):
    lane = lax.broadcasted_iota(jnp.int32, speed.shape, 1)
    first = lane < HALF
    angle = speed * turns + jnp.where(first, 0.25, 0.0)
    rest = angle - jnp.round(angle)
    square = rest * rest
    total = jnp.full_like(rest, SINE[-1])
    for term in SINE[-2::-1]:
        total = total * square + term
    wave = total * rest
    turned = pltpu.roll(wave, HALF, 1)
    return jnp.where(first, wave, turned), jnp.where(first, -turned, wave)


def rotate(weights, cosine, sine):
    return weights * cosine + pltpu.roll(weights, HALF, 1) * sine


def map_chunk(weights_ref, pair_ref, low_ref, into_ref):
    places, block, _ = weights_ref.shape
    high, low = split(weights_ref[...].reshape(places * block, LANES))
    both = jnp.concatenate([high, low], axis=1)
    width = 2 * LANES
    for column in range(0, pair_ref.shape[1], width):
        here = slice(column, column + width)
        total = dot(both, pair_ref[:, here]) + dot(high, low_ref[:, here])
        into_ref[:, :, here] = total.astype(BF16).reshape(places, block, width)


def last_kernel(done, weights, pair, low, out_hbm, rest, sems):
    ready = done.shape[1]
    block = weights.shape[2]
    copies = [
        pltpu.make_async_copy(done.at[place], out_hbm.at[place, pl.ds(0, ready)], sems.at[place])
        for place in range(GROUP)
    ]
    for copy in copies:
        copy.start()
    for index in range(CHUNKS - HERE):
        map_chunk(weights.at[HERE + index], pair, low, rest.at[index])
        copy = pltpu.make_async_copy(
            rest.at[index], out_hbm.at[:, pl.ds(ready + index * block, block)], sems.at[GROUP + index]
        )
        copy.start()
        copies.append(copy)
    for copy in copies:
        copy.wait()


def butterfly_kernel(
    rows, charges_hbm, speed_hbm, omega_hbm, mixers_hbm, source_hbm, target_hbm,
    out_ref, b_recv, target_pair, target_low,
    charges, omega, mixers, source, target, speeds, z_speeds, wide_t, source_pair, first_pair, high_mix, low_mix,
    speed_rows, tables, z_raw, z_send, z_recv, a_send, a_back, a_recv, b_send,
    t_in, t_out,
    load_sems, speed_sems, send_sems, z_raw_sem, z_recv_sems, a_back_sem, a_recv_sems, b_recv_sems, t_in_sem,
):
    per_peer = rows // GROUP
    block = per_peer // CHUNKS
    half = block // 2
    first_rows = Z_FIRST * block
    last_rows = T_LAST * half
    count = GROUP * block
    x_base, t_base = Z_FIRST * count, (Z_FIRST + X_COUNT) * count
    bx, by = lax.axis_index("bx"), lax.axis_index("by")
    z_count = lax.axis_size("bx") // 2
    y_count = lax.axis_size("by") // 2
    side = lax.rem(bx, 2)
    x_hi, x_lo, core = bx // z_count, by // y_count, lax.rem(by, 2)
    me = x_hi * 4 + core * 2 + x_lo
    across = 1 - 2 * side

    z_peer = {"bx": bx + across}
    peers = []
    cross = []
    for mask in PEER_ORDER:
        other_hi = lax.rem(x_hi + mask // 4, 2)
        other_core = lax.rem(core + mask // 2 % 2, 2)
        other_lo = lax.rem(x_lo + mask % 2, 2)
        to_bx = other_hi * z_count + lax.rem(bx, z_count)
        to_by = other_lo * y_count + (lax.rem(by, y_count) // 2) * 2 + other_core
        place = other_hi * 4 + other_core * 2 + other_lo
        peers.append(({"bx": to_bx, "by": to_by}, place))
        cross.append(({"bx": to_bx + across, "by": to_by}, place))
    cross.append((z_peer, me))

    barrier = pltpu.get_barrier_semaphore()
    for device, _ in cross + peers:
        pl.semaphore_signal(barrier, inc=1, device_id=device, device_id_type=MESH)

    loads = [
        pltpu.make_async_copy(speed_hbm.at[me], speeds.at[side, me], load_sems.at[0]),
        pltpu.make_async_copy(omega_hbm, omega, load_sems.at[1]),
        pltpu.make_async_copy(source_hbm, source, load_sems.at[2]),
        pltpu.make_async_copy(charges_hbm.at[:, pl.ds(0, first_rows)], charges, load_sems.at[3]),
        pltpu.make_async_copy(mixers_hbm, mixers, load_sems.at[4]),
        pltpu.make_async_copy(target_hbm, target, load_sems.at[5]),
        pltpu.make_async_copy(speed_hbm, z_speeds.at[0], load_sems.at[6]),
    ]
    for load in loads:
        load.start()

    def wait_bytes(ref, sem):
        pltpu.make_async_copy(ref, ref, sem).wait()

    def send(source_ref, target_ref, send_sem, recv_sem, device):
        pltpu.make_async_remote_copy(
            src_ref=source_ref, dst_ref=target_ref, send_sem=send_sem, recv_sem=recv_sem,
            device_id=device, device_id_type=MESH,
        ).start()

    def rows_of_chunk(chunk):
        return pl.ds(pl.multiple_of(chunk * block, block), block)

    def half_of(which):
        return pl.ds(pl.multiple_of(which * half, half), half)

    def turns_of(level):
        row = omega[pl.ds(level, 1), :] * (1.0 / (2.0 * math.pi))
        return jnp.concatenate([row, row], axis=1)

    def source_weights(value):
        high, low = split(value)
        both = dot(jnp.concatenate([high, low], axis=1), source_pair[...])
        return both[:, :LANES] + both[:, LANES:]

    def scatter_charges(slot):
        here = rows_of_chunk((T_CHUNKS + X_CHUNKS)[slot])
        for device, place in peers:
            send(charges_hbm.at[place, here], a_recv.at[slot, me], send_sems.at[0], a_recv_sems.at[slot], device)
        pltpu.make_async_copy(charges_hbm.at[me, here], a_recv.at[slot, me], a_recv_sems.at[slot]).start()

    pl.semaphore_wait(barrier, 2 * GROUP - 1)
    send(speed_hbm, z_speeds.at[1], speed_sems.at[0], speed_sems.at[1], z_peer)
    for device, place in peers:
        send(speed_hbm.at[place], speeds.at[side, me], speed_sems.at[2], speed_sems.at[3], device)
    for place in range(GROUP):
        here = pl.ds(0, first_rows)
        send(charges_hbm.at[place, here], z_raw.at[place], send_sems.at[1], z_raw_sem, z_peer)
    scatter_charges(0)

    loads[1].wait()
    loads[2].wait()
    high, low = split(source[...])
    source_pair[0:LANES, 0:LANES] = high
    source_pair[0:LANES, LANES:] = low
    source_pair[LANES:, 0:LANES] = high
    source_pair[LANES:, LANES:] = jnp.zeros_like(high)

    loads[4].wait()
    for child in range(2):
        span = slice(child * LANES, (child + 1) * LANES)
        high, low = split(mixers[0, side, lax.rem(side + child, 2)])
        first_pair[span, 0:LANES] = high
        first_pair[span, LANES:] = low
        for level in range(LEVELS):
            for target_half in range(2):
                high, low = split(mixers[level, target_half, child])
                place = (level, span, slice(target_half * LANES, (target_half + 1) * LANES))
                high_mix[place] = high
                low_mix[place] = low

    scatter_charges(1)

    loads[5].wait()
    high, low = split(target[...])
    target_pair[0:LANES, :] = high
    target_pair[LANES:, :] = high
    target_low[...] = low
    scatter_charges(2)

    def t_forward(index):
        here = pl.ds(index * half, half)
        wait_bytes(a_recv.at[index], a_recv_sems.at[index])
        for place in range(GROUP):
            send(
                a_recv.at[index, place, half_of(1 - side)], t_in.at[side, place, here],
                send_sems.at[2], t_in_sem, z_peer,
            )
        t_in[side, :, here, :] = a_recv[index, :, half_of(side), :]

    t_forward(0)
    loads[0].wait()
    wait_bytes(speeds.at[0, pl.ds(0, GROUP - 1)], speed_sems.at[3])
    send(speeds.at[side], speeds.at[side], speed_sems.at[4], speed_sems.at[5], z_peer)
    scatter_charges(3)

    def widen(into, columns):
        for place in range(GROUP):
            into[place] = jnp.broadcast_to(columns[:, place:place + 1], (columns.shape[0], LANES))

    groups = per_peer // LANES
    for group in range(groups):
        columns = jnp.transpose(speeds[side, :, group, :])
        for place in range(GROUP):
            if group == 0:
                speed_rows[place * first_rows:(place + 1) * first_rows] = jnp.broadcast_to(
                    columns[:first_rows, place:place + 1], (first_rows, LANES)
                )
            for index, chunk in enumerate(X_CHUNKS):
                start = chunk * block - group * LANES
                into = x_base + index * count + place * block
                if 0 <= start < LANES:
                    speed_rows[into:into + block] = jnp.broadcast_to(
                        columns[start:start + block, place:place + 1], (block, LANES)
                    )

    def fill_tables(first, blocks, levels):
        def body(index, carry):
            here = pl.ds(pl.multiple_of(first + index * count, count), count)
            for level in levels:
                cosine, sine = phase_tables(speed_rows[here, :], turns_of(level))
                tables[level, 0, here, :] = cosine
                tables[level, 1, here, :] = sine
            return carry

        lax.fori_loop(0, blocks, body, 0)

    for slot in range(4, T_LAST + X_COUNT):
        scatter_charges(slot)
    fill_tables(x_base, X_COUNT, range(LEVELS))
    for index in range(1, T_LAST):
        t_forward(index)
    fill_tables(0, Z_FIRST, range(1, LEVELS))

    def mix(rotated, level, stride, size):
        places = rotated.shape[0] // size
        low_places = [place for place in range(places) if place // stride % 2 == 0]

        def gather(shift):
            parts = [rotated[(place + shift) * size:(place + shift + 1) * size] for place in low_places]
            return jnp.concatenate(parts, axis=0)

        high, low = split(jnp.concatenate([gather(0), gather(stride)], axis=1))
        both = dot(jnp.concatenate([high, low], axis=0), high_mix[level])
        count = high.shape[0]
        mixed = both[:count] + both[count:] + dot(high, low_mix[level])
        parts = [None] * places
        for index, place in enumerate(low_places):
            taken = mixed[index * size:(index + 1) * size]
            parts[place] = taken[:, :LANES]
            parts[place + stride] = taken[:, LANES:]
        return jnp.concatenate(parts, axis=0)

    def turned(weights, level, here):
        return rotate(weights, tables[level, 0, here, :], tables[level, 1, here, :])

    def other_levels(weights, here, size):
        for level in range(1, LEVELS):
            weights = mix(turned(weights, level, here), level, {1: 4, 2: 2, 3: 1}[level], size)
        return weights

    def first_level(own, other):
        high, low = split(jnp.concatenate([own, other], axis=1))
        both = dot(high, first_pair[...])
        return both[:, :LANES] + both[:, LANES:] + dot(low, first_pair[:, :LANES])

    def x_rows(index):
        return pl.ds(pl.multiple_of(x_base + index * count, count), count)

    def x_first_start(index, carry):
        slot = index + T_LAST
        wait_bytes(a_recv.at[slot], a_recv_sems.at[slot])
        weights = source_weights(a_recv[slot].reshape(count, LANES))
        z_send[index] = turned(weights, 0, x_rows(index)).reshape(GROUP, block, LANES)
        for place in range(GROUP):
            send(z_send.at[index, place], z_recv.at[index, place], send_sems.at[3], z_recv_sems.at[index], z_peer)
        return carry

    def give_back(slot, chunk):
        for device, place in peers:
            send(b_send.at[slot, place], b_recv.at[chunk, me], send_sems.at[4], b_recv_sems.at[chunk], device)
        pltpu.make_async_copy(b_send.at[slot, me], b_recv.at[chunk, me], b_recv_sems.at[chunk]).start()

    def t_back_across(devices):
        for device in devices:
            for piece in range(T_LAST):
                t_back(piece, 1 - side, [device], send_sems.at[7])

    def x_first_end(index, carry):
        @pl.when(index == RETURN_AT)
        def _():
            t_back_across(cross[:2])

        wait_bytes(z_recv.at[index], z_recv_sems.at[index])

        @pl.when(index == RETURN_AT)
        def _():
            t_back_across(cross[2:])

        weights = first_level(z_send[index].reshape(count, LANES), z_recv[index].reshape(count, LANES))
        weights = other_levels(weights, x_rows(index), block)
        slot = Z_FIRST + index
        b_send[slot] = weights.reshape(GROUP, block, LANES)
        give_back(slot, slot + (X_CHUNKS[-1] - X_CHUNKS[-2] - 1) * (index // (X_COUNT - 1)))
        return carry

    def targets(chunk, carry):
        wait_bytes(b_recv.at[chunk], b_recv_sems.at[chunk])
        map_chunk(b_recv.at[chunk], target_pair, target_low, out_ref.at[:, rows_of_chunk(chunk), :])
        return carry

    loads[3].wait()
    loads[6].wait()
    wait_bytes(z_speeds.at[1], speed_sems.at[1])
    wait_bytes(z_raw, z_raw_sem)
    first_count = GROUP * first_rows
    sides = []
    for index, value in enumerate((charges, z_raw)):
        columns = jnp.transpose(z_speeds[index, :, 0, :])
        speed_here = jnp.concatenate(
            [
                jnp.broadcast_to(columns[:first_rows, place:place + 1], (first_rows, LANES))
                for place in range(GROUP)
            ],
            axis=0,
        )
        cosine, sine = phase_tables(speed_here, turns_of(0))
        sides.append(rotate(source_weights(value[...].reshape(first_count, LANES)), cosine, sine))
    a_send[...] = first_level(*sides).reshape(GROUP, first_rows, LANES)
    for device, place in peers:
        send(a_send.at[place], a_back.at[me], send_sems.at[5], a_back_sem, device)
    pltpu.make_async_copy(a_send.at[me], a_back.at[me], a_back_sem).start()

    x_first_start(0, 0)

    wait_bytes(speeds.at[0], speed_sems.at[5])
    for plane in range(2):
        columns = jnp.transpose(speeds[plane, :, groups - 1, :])
        widen(wide_t.at[plane], columns)
    for plane in range(2):
        for place in range(GROUP):
            for piece, chunk in enumerate(T_CHUNKS):
                start = pl.multiple_of(chunk * block - (groups - 1) * LANES + side * half, half)
                into = t_base + (plane * GROUP + place) * last_rows + piece * half
                speed_rows[into:into + half] = wide_t[plane, place, pl.ds(start, half), :]
    fill_tables(t_base, T_LAST, range(LEVELS))
    lax.fori_loop(1, X_COUNT, x_first_start, 0)
    wait_bytes(t_in.at[0], t_in_sem)
    weights = source_weights(t_in[...].reshape(2 * GROUP * last_rows, LANES))
    t_rows = slice(t_base, t_base + 2 * GROUP * last_rows)
    weights = mix(turned(weights, 0, t_rows), 0, GROUP, last_rows)
    weights = other_levels(weights, t_rows, last_rows)
    t_out[...] = weights.reshape(2, GROUP, last_rows, LANES)

    def t_back(index, plane, devices, sem):
        chunk = T_CHUNKS[index]
        here = pl.ds(index * half, half)
        for device, place in devices:
            send(
                t_out.at[plane, place, here], b_recv.at[chunk, me, half_of(side)],
                sem, b_recv_sems.at[chunk], device,
            )

    for index in range(T_LAST):
        t_back(index, side, peers, send_sems.at[6])
        pltpu.make_async_copy(
            t_out.at[side, me, pl.ds(index * half, half)],
            b_recv.at[T_CHUNKS[index], me, half_of(side)],
            b_recv_sems.at[T_CHUNKS[index]],
        ).start()

    wait_bytes(a_back, a_back_sem)
    weights = other_levels(a_back[...].reshape(first_count, LANES), slice(0, x_base), first_rows)
    for chunk in range(Z_FIRST):
        b_send[chunk] = weights.reshape(GROUP, first_rows, LANES)[:, chunk * block:(chunk + 1) * block, :]
        give_back(chunk, chunk)

    lax.fori_loop(0, X_COUNT, x_first_end, 0)
    lax.fori_loop(0, HERE, targets, 0)
    for chunk in range(HERE, CHUNKS):
        wait_bytes(b_recv.at[chunk], b_recv_sems.at[chunk])

    most = pl.ds(0, GROUP - 1)
    wait_bytes(a_recv.at[:, most], send_sems.at[0])
    wait_bytes(z_raw, send_sems.at[1])
    wait_bytes(t_in.at[0], send_sems.at[2])
    wait_bytes(z_recv, send_sems.at[3])
    wait_bytes(b_send.at[:, most], send_sems.at[4])
    wait_bytes(a_back.at[most], send_sems.at[5])
    wait_bytes(t_in.at[0, most], send_sems.at[6])
    wait_bytes(t_in.at[0], send_sems.at[7])
    wait_bytes(z_speeds.at[1], speed_sems.at[0])
    wait_bytes(speeds.at[0, most], speed_sems.at[2])
    wait_bytes(speeds.at[0], speed_sems.at[4])


def shards(charges, speed, omega, mixers, source_map, target_map):
    rows, targets = charges.shape[2], target_map.shape[1]
    per_peer = rows // GROUP
    block = per_peer // CHUNKS
    first_rows, last_rows = Z_FIRST * block, T_LAST * block // 2
    whole = (GROUP, per_peer, LANES)
    lines = (GROUP, per_peer // LANES, LANES)
    square = (2 * LANES, 2 * LANES)
    dma = pltpu.SemaphoreType.DMA
    operands = [charges.reshape(whole), speed.reshape(lines), omega, mixers, source_map, target_map]
    done, weights, pair, low = pl.pallas_call(
        functools.partial(butterfly_kernel, rows),
        name="butterfly",
        out_shape=(
            pltpu.VMEM((GROUP, HERE * block, targets), BF16),
            pltpu.VMEM((CHUNKS, GROUP, block, LANES), F32),
            pltpu.VMEM((2 * LANES, targets), BF16),
            pltpu.VMEM((LANES, targets), BF16),
        ),
        in_specs=[pl.BlockSpec(memory_space=pltpu.HBM)] * len(operands),
        out_specs=(pl.BlockSpec(memory_space=pltpu.VMEM),) * 4,
        scratch_shapes=[
            pltpu.VMEM((GROUP, first_rows, LANES), F32),
            pltpu.VMEM((LEVELS, HALF), F32),
            pltpu.VMEM((LEVELS, 2, 2, LANES, LANES), F32),
            pltpu.VMEM((LANES, LANES), F32),
            pltpu.VMEM((LANES, targets), F32),
            pltpu.VMEM((2,) + lines, F32),
            pltpu.VMEM((2,) + lines, F32),
            pltpu.VMEM((2, GROUP, LANES, LANES), F32),
            pltpu.VMEM(square, BF16),
            pltpu.VMEM(square, BF16),
            pltpu.VMEM((LEVELS,) + square, BF16),
            pltpu.VMEM((LEVELS,) + square, BF16),
            pltpu.VMEM((rows, LANES), F32),
            pltpu.VMEM((LEVELS, 2, rows, LANES), F32),
            pltpu.VMEM((GROUP, first_rows, LANES), F32),
            pltpu.VMEM((X_COUNT, GROUP, block, LANES), F32),
            pltpu.VMEM((X_COUNT, GROUP, block, LANES), F32),
            pltpu.VMEM((GROUP, first_rows, LANES), F32),
            pltpu.VMEM((GROUP, first_rows, LANES), F32),
            pltpu.VMEM((CHUNKS - Z_FIRST, GROUP, block, LANES), F32),
            pltpu.VMEM((CHUNKS - T_LAST, GROUP, block, LANES), F32),
            pltpu.VMEM((2, GROUP, last_rows, LANES), F32),
            pltpu.VMEM((2, GROUP, last_rows, LANES), F32),
            dma((7,)),
            dma((6,)),
            dma((8,)),
            dma,
            dma((X_COUNT,)),
            dma,
            dma((CHUNKS - Z_FIRST,)),
            dma((CHUNKS,)),
            dma,
        ],
        compiler_params=pltpu.CompilerParams(
            collective_id=0, has_side_effects=True, vmem_limit_bytes=VMEM_LIMIT
        ),
    )(*[pltpu.with_memory_space_constraint(operand, pltpu.HBM) for operand in operands])
    parts = [pltpu.with_memory_space_constraint(part, pltpu.VMEM) for part in (done, weights, pair, low)]
    result = pl.pallas_call(
        last_kernel,
        name="last",
        out_shape=jax.ShapeDtypeStruct((GROUP, per_peer, targets), BF16),
        in_specs=[pl.BlockSpec(memory_space=pltpu.VMEM)] * 4,
        out_specs=pl.BlockSpec(memory_space=pl.ANY),
        scratch_shapes=[pltpu.VMEM((CHUNKS - HERE, GROUP, block, targets), BF16), dma((GROUP + CHUNKS - HERE,))],
        compiler_params=pltpu.CompilerParams(vmem_limit_bytes=8 * 2**20),
    )(*parts)
    return result.reshape(1, 1, rows, targets)


def solution(mesh):
    placed = (P("bx", "by", None, None), P("bx", "by", None), P(), P(), P(), P())
    return jax.shard_map(
        shards, mesh=mesh, in_specs=placed, out_specs=P("bx", "by", None, None), check_vma=False
    )
```
